128 devices in a mesh: fsdp: 16 (over z_hi, y, core), tp: 8 (over x, z_lo).
Axes of the slice: x: 4, y: 4, z: 4 (z_hi: 2, z_lo: 2; z = z_hi * 2 + z_lo), core: 2. Of those that a mesh axis runs over, the one named last changes fastest.
Arguments:
- tokens: bfloat16 [16384, 7168], P('fsdp', 'tp'), may hold values from -200 to 200
- gain: float32 [7168], P('tp'), may hold values from 0.1 to 1.9
- rollout_weight: bfloat16 [7168, 9216], P(None, 'tp'), may hold values from -0.0625 to 0.0625
- delta_values: bfloat16 [7168, 9216], P(('fsdp', 'tp')), may hold values from -6 to 6
- scale_exponents: int32 [7168, 72], P(('fsdp', 'tp')), may hold values from -8 to -5
Outputs:
- activated: bfloat16 [16384, 9216], P('fsdp', 'tp')
The draws below stay inside these ranges and needn't reach their ends.
All inputs are finite; a program needn't handle non-finite values.
Results may differ from the reference program's by a relative error of at most 0.015.
Values may be sent and summed in bfloat16 or wider, within the bound.
No kernel may reach another device: no remote copies, remote signals or barrier semaphores. Data moves between devices by JAX's collectives and lax.ppermute only.
A program may use at most 256 MiB of HBM per device.

```python
import jax
import jax.numpy as jnp
from jax import lax

D = 7168
FW = 9216
GROUP = 128
TOKENS = 16384


def draw_tokens(key, part):
    key = jax.random.fold_in(key, 11)
    first, second, third = jax.random.split(key, 3)
    rising = jnp.exp(jnp.log(3.0) * jnp.arange(D, dtype=jnp.float32) / (D - 1))
    columns = jnp.exp(jax.random.uniform(second, (1, D), jnp.float32, 0.0, jnp.log(10.0))) * rising[None, :]
    rows = jnp.exp(jax.random.uniform(third, (TOKENS, 1), jnp.float32, 0.0, jnp.log(10.0)))
    base = jnp.clip(jax.random.normal(first, (TOKENS, D), jnp.float32), -6.0, 6.0)
    return (base * columns * rows / 10.0).astype(jnp.bfloat16)


def touch_ends(result, key, smallest, high):
    longest = result.shape.index(max(result.shape))
    spots = []
    for shift in (0, 1):
        where = [jax.random.randint(jax.random.fold_in(key, axis), (), 0, length) for axis, length in enumerate(result.shape)]
        where[longest] = (where[longest] + shift) % result.shape[longest]
        spots.append(tuple(where))
    return result.at[spots[0]].set(smallest).at[spots[1]].set(high)


def steps_of(rng, extent, cuts, least, high):
    factor_of = 1.0
    for axis_at, shards_of in cuts:
        heights = jax.random.uniform(jax.random.fold_in(jax.random.fold_in(rng, 6), axis_at), (shards_of,), jnp.float32, least / len(cuts), high / len(cuts))
        factor_of = factor_of * jnp.repeat(jnp.exp(heights), extent[axis_at] // shards_of).reshape((-1,) + (1,) * (len(extent) - 1 - axis_at))
    return factor_of


def bell_draw(stream_key, extent, scale, most, shards=(), kind=jnp.bfloat16):
    level = steps_of(stream_key, extent, shards, -0.22, 0.18) if shards else 1.0
    entries = jax.random.normal(stream_key, extent, jnp.float32) * scale * level
    return jnp.minimum(jnp.maximum(entries, -most), most).astype(kind)


def setup_inputs(seed: int = 0) -> dict:
    arg_keys = jax.random.split(jax.random.key(seed), 6)
    return {
        "tokens": draw_tokens(jax.random.fold_in(arg_keys[5], 71), 0),
        "gain": jnp.clip(1.0 + 0.18 * jax.random.normal(arg_keys[1], (D,), jnp.float32), 0.1, 1.9),
        "rollout_weight": bell_draw(arg_keys[2], (D, FW), D ** -0.5, 0.0625, ((1, 8),)),
        "delta_values": bell_draw(arg_keys[3], (D, FW), 1.0, 6.0, ((0, 128),)),
        "scale_exponents": touch_ends(jax.random.randint(arg_keys[4], (D, FW // GROUP), -8, -4), jax.random.fold_in(arg_keys[4], 1), -8, (-4) - 1).astype(jnp.int32),
    }


def power_two(exps):
    total = jnp.zeros(exps.shape, jnp.float32)
    for level in range(-8, -4):
        total = total + jnp.where(exps == level, jnp.float32(2.0 ** level), jnp.float32(0.0))
    return total

def reference(tokens, gain, rollout_weight, delta_values, scale_exponents):
    scale = jnp.repeat(power_two(scale_exponents), GROUP, axis=1)
    refreshed = (rollout_weight.astype(jnp.float32) + delta_values.astype(jnp.float32) * scale).astype(jnp.bfloat16)
    x = tokens.astype(jnp.float32)
    power = lax.optimization_barrier(jnp.mean(x * x, axis=1, keepdims=True))
    normed = (x * lax.rsqrt(power + 1e-06) * gain[None, :]).astype(jnp.bfloat16)
    hidden = jnp.dot(normed, refreshed, preferred_element_type=jnp.float32)
    return jax.nn.silu(hidden).astype(jnp.bfloat16)
```

```python
import functools

import jax
import jax.numpy as jnp
from jax import lax
from jax.experimental import pallas as pl
from jax.experimental.pallas import tpu as pltpu
from jax.sharding import PartitionSpec as P


def links(x=0, z_lo=0, z_hi=0, y=0, core=0):
    pairs = []
    for f in range(16):
        for t in range(8):
            f2 = (((f // 8) + z_hi) % 2) * 8 + (((f // 2) % 4 + y) % 4) * 2 + (f + core) % 2
            t2 = ((t // 2 + x) % 4) * 2 + (t + z_lo) % 2
            pairs.append((f * 8 + t, f2 * 8 + t2))
    return pairs


def shift(value, **step):
    return lax.ppermute(value, ("fsdp", "tp"), links(**step))


def power_two(exps):
    total = jnp.zeros(exps.shape, jnp.float32)
    for level in range(-8, -4):
        total = total + jnp.where(exps == level, jnp.float32(2.0**level), jnp.float32(0.0))
    return total


def scale_kernel(place, exps, delta, *outs):
    groups = exps.shape[1]
    scale = power_two(exps[...])
    x, z_lo = place[0], place[1]
    width = outs[0].shape[2]
    per = width // 128
    scaled = []
    for owner in range(8):
        columns = []
        for g in range(per):
            at = owner * per + g
            piece = delta[:, at * 128 : (at + 1) * 128].astype(jnp.float32) * scale[:, at : at + 1]
            columns.append(piece.astype(jnp.bfloat16))
        block = jnp.concatenate(columns, axis=1)
        j = lax.rem(owner // 2 - x + 4, 4)
        half = jnp.where(z_lo == owner % 2, 0, 1)
        for k in range(4):
            @pl.when(j == k)
            def _(k=k, block=block, half=half):
                outs[k][half] = block


def scaled_delta(place, exps, delta):
    rows, wide = delta.shape
    width = wide // 8
    return pl.pallas_call(
        scale_kernel,
        out_shape=[jax.ShapeDtypeStruct((2, rows, width), jnp.bfloat16)] * 4,
        in_specs=[
            pl.BlockSpec(memory_space=pltpu.SMEM),
            pl.BlockSpec(memory_space=pltpu.VMEM),
            pl.BlockSpec(memory_space=pltpu.VMEM),
        ],
        out_specs=[pl.BlockSpec(memory_space=pltpu.VMEM)] * 4,
        name="scaled_delta",
    )(place, exps, delta)


def refresh_kernel(place, same, other, base, out):
    x, z_lo = place[0], place[1]
    for t in range(8):
        j = lax.rem(x - t // 2 + 4, 4)
        delta = jnp.where(z_lo == t % 2, same[j].astype(jnp.float32), other[j].astype(jnp.float32))
        out[t] = (base[t].astype(jnp.float32) + delta).astype(jnp.bfloat16)


def refresh(place, same, other, base, name):
    return pl.pallas_call(
        refresh_kernel,
        out_shape=jax.ShapeDtypeStruct(base.shape, jnp.bfloat16),
        in_specs=[pl.BlockSpec(memory_space=pltpu.SMEM)] + [pl.BlockSpec(memory_space=pltpu.VMEM)] * 3,
        out_specs=pl.BlockSpec(memory_space=pltpu.VMEM),
        name=name,
    )(place, same, other, base)


def gate(*values):
    return lax.optimization_barrier(values)


def assemble_kernel(spots, place, *refs):
    count = len(spots)
    pieces, out, held, sem, out_sem = refs[:count], refs[count], refs[count + 1], refs[count + 2], refs[count + 3]
    y, z_hi, core = place[2], place[3], place[4]
    full = out.shape[0] // 16
    copies = []
    for at, (step, other_core, other_hi) in enumerate(spots):
        y2 = lax.rem(y + step + 4, 4)
        hi = lax.rem(z_hi + other_hi, 2)
        c = lax.rem(core + other_core, 2)
        row = pl.multiple_of((hi * 8 + y2 * 2 + c) * full, 16)
        copy = pltpu.make_async_copy(pieces[at], held.at[pl.ds(row, full)], sem.at[at])
        copy.start()
        copies.append(copy)
    for copy in copies:
        copy.wait()
    copy = pltpu.make_async_copy(held, out, out_sem)
    copy.start()
    copy.wait()


def assemble(place, pieces, spots):
    full, width = pieces[0].shape
    count = len(pieces)
    return pl.pallas_call(
        functools.partial(assemble_kernel, spots),
        out_shape=jax.ShapeDtypeStruct((full * 16, width), jnp.bfloat16),
        in_specs=[pl.BlockSpec(memory_space=pltpu.SMEM)] + [pl.BlockSpec(memory_space=pl.ANY)] * count,
        out_specs=pl.BlockSpec(memory_space=pl.ANY),
        scratch_shapes=[
            pltpu.VMEM((full * 16, width), jnp.bfloat16),
            pltpu.SemaphoreType.DMA((count,)),
            pltpu.SemaphoreType.DMA,
        ],
        compiler_params=pltpu.CompilerParams(vmem_limit_bytes=30 * 2**20),
        cost_estimate=pl.CostEstimate(flops=0, bytes_accessed=64 * full * width, transcendentals=0),
        name="assemble_weight",
    )(place, *pieces)


STEPS = (0, -1, 1, 2)
TILE = 256


def product_kernel(spots, start, fresh_out, place, *refs):
    count = len(spots)
    pieces, inv, w = refs[:count], refs[count], refs[count + 1]
    out, xbuf, wbuf, acc, result, xsem, wsem, osem = refs[count + (2 if fresh_out else 3) :]
    x, z_lo = place[0], place[1]
    depth = wbuf.shape[1]
    rows = acc.shape[0]
    waits = [[], [], [], []]
    for j in range(4):
        for at, (k, row, column) in enumerate(spots):
            if k != j:
                continue
            ref = pieces[at]
            target = xbuf.at[j, pl.ds(row, ref.shape[0])]
            if column is not None:
                half = depth // 2
                side = jnp.where(z_lo == 0, column, 1 - column)
                target = xbuf.at[j, pl.ds(row, ref.shape[0]), pl.ds(pl.multiple_of(side * half, 128), half)]
            copy = pltpu.make_async_copy(ref, target, xsem.at[at])
            copy.start()
            waits[j].append(copy)
        block = pl.multiple_of(lax.rem(x + STEPS[j] + 4, 4) * depth, 16)
        copy = pltpu.make_async_copy(w.at[pl.ds(block, depth)], wbuf.at[j], wsem.at[j])
        copy.start()
        waits[j].append(copy)
    for j in range(4):
        for copy in waits[j]:
            copy.wait()

        @pl.loop(0, rows // TILE)
        def _(i, j=j):
            here = pl.ds(pl.multiple_of(i * TILE, TILE), TILE)
            part = jnp.dot(xbuf[j, here], wbuf[j], preferred_element_type=jnp.float32)
            if j == 0:
                acc[here] = part
            elif j < 3:
                acc[here] += part
            else:
                hidden = (acc[here] + part) * inv[here]
                result[here] = (hidden / (1.0 + jnp.exp(-hidden))).astype(result.dtype)

    copy = pltpu.make_async_copy(result, out.at[pl.ds(start, rows)], osem)
    copy.start()
    copy.wait()


def product(place, pieces, spots, inv, w, start, total, out, name):
    rows = inv.shape[0]
    depth, width = w.shape[0] // 4, w.shape[1]
    anywhere = pl.BlockSpec(memory_space=pl.ANY)
    vmem = pl.BlockSpec(memory_space=pltpu.VMEM)
    count = len(pieces)
    operands = [place, *pieces, inv, w] + ([] if out is None else [out])
    return pl.pallas_call(
        functools.partial(product_kernel, spots, start, out is None),
        out_shape=jax.ShapeDtypeStruct((total, width), jnp.bfloat16),
        in_specs=[pl.BlockSpec(memory_space=pltpu.SMEM)]
        + [anywhere] * count
        + [vmem, anywhere]
        + ([] if out is None else [anywhere]),
        out_specs=anywhere,
        input_output_aliases={} if out is None else {count + 3: 0},
        scratch_shapes=[
            pltpu.VMEM((4, rows, depth), jnp.bfloat16),
            pltpu.VMEM((4, depth, width), jnp.bfloat16),
            pltpu.VMEM((rows, width), jnp.float32),
            pltpu.VMEM((rows, width), jnp.bfloat16),
            pltpu.SemaphoreType.DMA((count,)),
            pltpu.SemaphoreType.DMA((4,)),
            pltpu.SemaphoreType.DMA,
        ],
        compiler_params=pltpu.CompilerParams(vmem_limit_bytes=50 * 2**20),
        cost_estimate=pl.CostEstimate(
            flops=2 * rows * 4 * depth * width,
            bytes_accessed=2 * (4 * depth * (rows + width) + rows * width),
            transcendentals=rows * width,
        ),
        name=name,
    )(*operands)


def local(tokens, gain, rollout_weight, delta_values, scale_exponents):
    f, t = lax.axis_index("fsdp"), lax.axis_index("tp")
    x, z_lo = t // 2, t % 2
    z_hi, y, core = f // 8, (f // 2) % 4, f % 2
    place = jnp.stack([x, z_lo, y, z_hi, core]).astype(jnp.int32)
    count, features = tokens.shape
    total = features * 8
    block = rollout_weight.shape[0] // 16

    values = tokens.astype(jnp.float32)
    scaled = (values * gain[None, :]).astype(jnp.bfloat16)
    square = jnp.sum(values * values, axis=1)
    rows = count // 4
    mine = [scaled[m * rows : (m + 1) * rows] for m in (0, 1, 3)]
    last = scaled[2 * rows : 3 * rows]
    half = rows // 2

    def pair(m, theirs):
        return jnp.where(
            z_lo == 0,
            jnp.concatenate([mine[m], theirs], axis=1),
            jnp.concatenate([theirs, mine[m]], axis=1),
        )

    parts = scaled_delta(place, scale_exponents, delta_values)
    got = [parts[0]] + [shift(parts[j], x=j) for j in (1, 2, 3)]
    left_c, right_c = shift(last, x=1), shift(last, x=-1)
    theirs = [shift(mine[0], z_lo=1), shift(mine[1], z_lo=1)]

    got[1], got[2], got[3], theirs[0] = gate(got[1], got[2], got[3], theirs[0])
    same = jnp.stack([g[0] for g in got])
    other = jnp.stack([g[1] for g in got])
    near = shift(other, z_lo=1)
    across = shift(other, z_lo=1, z_hi=1)
    far = shift(same, z_hi=1)
    pairs = [pair(0, theirs[0])]
    left, right = [shift(pairs[0], x=1)], [shift(pairs[0], x=-1)]
    base = rollout_weight.reshape(16, 8, block // 8, rollout_weight.shape[1])
    base_own = lax.dynamic_index_in_dim(base, f, 0, keepdims=False)
    base_far = lax.dynamic_index_in_dim(base, (f + 8) % 16, 0, keepdims=False)
    near, theirs[1], left_c, right_c = gate(near, theirs[1], left_c, right_c)
    fresh_own = refresh(place, same, near, base_own, "refresh_own").reshape(block, -1)

    pairs.append(pair(1, theirs[1]))
    left.append(shift(pairs[1], x=1))
    right.append(shift(pairs[1], x=-1))
    own_left, own_right = shift(fresh_own, y=1), shift(fresh_own, y=-1)
    far_ca, far_cb = shift(left_c[:half], x=1), shift(right_c[half:], x=-1)
    theirs.append(shift(mine[2], z_lo=1))
    theirs_c = shift(last, z_lo=1)

    far, across, left[0], right[0], theirs[2] = gate(far, across, left[0], right[0], theirs[2])
    fresh_far = refresh(place, far, across, base_far, "refresh_far").reshape(block, -1)
    far_left, far_right = shift(fresh_far, y=1), shift(fresh_far, y=-1)
    pairs.append(pair(2, theirs[2]))
    left.append(shift(pairs[2], x=1))
    right.append(shift(pairs[2], x=-1))
    theirs_l, theirs_r = shift(left_c, z_lo=1), shift(right_c, z_lo=1)

    own_left, own_right, left[1], right[1], left[0], far_ca, far_cb = gate(
        own_left, own_right, left[1], right[1], left[0], far_ca, far_cb
    )
    own_opposite = shift(own_left, y=1)
    opposite_0 = shift(left[0], x=1)
    opposite_1 = shift(right[1], x=-1)
    theirs_fa, theirs_fb = shift(far_ca, z_lo=1), shift(far_cb, z_lo=1)

    far_left, far_right, left[2], right[2], own_left = gate(far_left, far_right, left[2], right[2], own_left)
    far_opposite = shift(far_right, y=-1)
    opposite_2a = shift(left[2][:half], x=1)
    opposite_2b = shift(right[2][half:], x=-1)

    rings = [[fresh_own, own_left, own_right, own_opposite], [fresh_far, far_left, far_right, far_opposite]]
    pieces, spots = [], []
    for hi, ring in enumerate(rings):
        for step, piece in zip(STEPS, ring):
            pieces += [piece, shift(piece, core=1)]
            spots += [(step, 0, hi), (step, 1, hi)]
    weight = assemble(place, pieces, spots)

    for step in ({"z_lo": 1}, {"x": 1}, {"x": 2}):
        square = square + shift(square, **step)
    inv = lax.rsqrt(square / total + 1e-06)[:, None]

    tokens_a = [pairs[0], left[0], right[0], opposite_0, pairs[1], left[1], right[1], opposite_1]
    spots_a = [(j, m * rows, None) for m in (0, 1) for j in range(4)]
    tokens_a += [last, theirs_c, left_c, theirs_l, right_c, theirs_r, far_ca, theirs_fa, far_cb, theirs_fb]
    at = 2 * rows
    spots_a += [(j, at, side) for j in range(3) for side in (0, 1)]
    spots_a += [(3, at, 0), (3, at, 1), (3, at + half, 0), (3, at + half, 1)]
    first = product(place, tokens_a, spots_a, inv[: 3 * rows], weight, 0, count, None, "product_a")
    tokens_b = [pairs[2], left[2], right[2], opposite_2a, opposite_2b]
    spots_b = [(0, 0, None), (1, 0, None), (2, 0, None), (3, 0, None), (3, half, None)]
    return product(
        place, tokens_b, spots_b, inv[3 * rows :], weight, 3 * rows, count, first, "product_b"
    )


def solution(mesh):
    in_specs = (
        P("fsdp", "tp"),
        P("tp"),
        P(None, "tp"),
        P(("fsdp", "tp"), None),
        P(("fsdp", "tp"), None),
    )
    out_specs = P("fsdp", "tp")
    return jax.shard_map(local, mesh=mesh, in_specs=in_specs, out_specs=out_specs, check_vma=False)
```

```python
import functools

import jax
import jax.numpy as jnp
from jax import lax
from jax.experimental import pallas as pl
from jax.experimental.pallas import tpu as pltpu
from jax.sharding import PartitionSpec as P


SCOPED = 60 * 2**20
FREE = pl.CostEstimate(flops=0, bytes_accessed=0, transcendentals=0)


def links(x=0, z_lo=0, z_hi=0, y_by_core=0, core=0):
    pairs = []
    for f in range(16):
        for t in range(8):
            along = y_by_core if f % 2 == 0 else -y_by_core
            f2 = (((f // 8) + z_hi) % 2) * 8 + (((f // 2) % 4 + along) % 4) * 2 + (f + core) % 2
            t2 = ((t // 2 + x) % 4) * 2 + (t + z_lo) % 2
            pairs.append((f * 8 + t, f2 * 8 + t2))
    return pairs


def shift(value, **step):
    return lax.ppermute(value, ("fsdp", "tp"), links(**step))


def position():
    f, t = lax.axis_index("fsdp"), lax.axis_index("tp")
    return t // 2, t % 2, (f // 2) % 4, f // 8, f % 2


def power_two(exps):
    total = jnp.zeros(exps.shape, jnp.float32)
    for level in range(-8, -4):
        total = total + jnp.where(exps == level, jnp.float32(2.0**level), jnp.float32(0.0))
    return total


def scale_kernel(exps, delta, *outs):
    groups = exps.shape[1]
    scale = power_two(exps[...])
    x, z_lo, _, _, _ = position()
    width = outs[0].shape[2]
    per = width // 128
    scaled = []
    for owner in range(8):
        columns = []
        for g in range(per):
            at = owner * per + g
            piece = delta[:, at * 128 : (at + 1) * 128].astype(jnp.float32) * scale[:, at : at + 1]
            columns.append(piece.astype(jnp.bfloat16))
        block = jnp.concatenate(columns, axis=1)
        j = lax.rem(owner // 2 - x + 4, 4)
        half = jnp.where(z_lo == owner % 2, 0, 1)
        for k in range(4):
            @pl.when(j == k)
            def _(k=k, block=block, half=half):
                outs[k][half] = block


def scaled_delta(exps, delta):
    rows, wide = delta.shape
    width = wide // 8
    return pl.pallas_call(
        scale_kernel,
        out_shape=[jax.ShapeDtypeStruct((2, rows, width), jnp.bfloat16)] * 4,
        in_specs=[pl.BlockSpec(memory_space=pltpu.VMEM)] * 2,
        out_specs=[pl.BlockSpec(memory_space=pltpu.VMEM)] * 4,
        compiler_params=pltpu.CompilerParams(vmem_limit_bytes=SCOPED),
        cost_estimate=FREE,
        name="scaled_delta",
    )(exps, delta)


def refresh_kernel(other_hi, same, other, base, out, held, sem):
    x, z_lo, y, z_hi, core = position()
    owner = lax.rem(z_hi + other_hi, 2) * 8 + y * 2 + core
    copy = pltpu.make_async_copy(base.at[pl.ds(owner * 8, 8)], held, sem)
    copy.start()
    copy.wait()
    for t in range(8):
        j = lax.rem(x - t // 2 + 4, 4)
        delta = jnp.where(z_lo == t % 2, same[j].astype(jnp.float32), other[j].astype(jnp.float32))
        out[t] = (held[t].astype(jnp.float32) + delta).astype(jnp.bfloat16)


def refresh(same, other, base, other_hi, name):
    shape = (8, *base.shape[1:])
    vmem = pl.BlockSpec(memory_space=pltpu.VMEM)
    out = pl.pallas_call(
        functools.partial(refresh_kernel, other_hi),
        out_shape=jax.ShapeDtypeStruct(shape, jnp.bfloat16),
        in_specs=[vmem, vmem, pl.BlockSpec(memory_space=pltpu.HBM)],
        out_specs=vmem,
        scratch_shapes=[pltpu.VMEM(shape, jnp.bfloat16), pltpu.SemaphoreType.DMA],
        compiler_params=pltpu.CompilerParams(vmem_limit_bytes=SCOPED),
        cost_estimate=FREE,
        name=name,
    )(same, other, base)
    return out.reshape(8 * shape[1], shape[2])


def gate(*values):
    return lax.optimization_barrier(values)


STEPS = (0, -1, 1, 2)
TILE = 256
HBM = pl.BlockSpec(memory_space=pltpu.HBM)
VMEM = pl.BlockSpec(memory_space=pltpu.VMEM)


def silu(hidden):
    return hidden / (1.0 + jnp.exp(-hidden))


def start_weights(block, held, pieces, spots, sem):
    _, _, y, z_hi, core = position()
    piece = held.shape[0] // 4
    for which, index, step, other_core, other_hi in spots:
        y2 = lax.rem(y + jnp.where(core == 0, step, -step) + 4, 4)
        part = lax.rem(y2, 2) * 2 + lax.rem(core + other_core, 2)

        @pl.when(lax.rem(z_hi + other_hi, 2) * 2 + y2 // 2 == block)
        def _(which=which, index=index, part=part):
            source = pieces[which] if index is None else pieces[which].at[index]
            target = held.at[pl.ds(pl.multiple_of(part * piece, 16), piece)]
            pltpu.make_async_copy(source, target, sem).start()


def start_tokens(held, pieces, spots, sem):
    z_lo = position()[1]
    half = held.shape[1] // 2
    for which, row, side, first, size in spots:
        column = jnp.where(z_lo == 0, side, 1 - side)
        target = held.at[pl.ds(row, size), pl.ds(pl.multiple_of(column * half, 128), half)]
        pltpu.make_async_copy(pieces[which].at[pl.ds(first, size)], target, sem).start()


def wait_all(held, sem):
    pltpu.make_async_copy(held, held, sem).wait()


def product_kernel(own_half, n_tok, n_wt, token_spots, weight_spots, *refs):
    tokens, weights = refs[:n_tok], refs[n_tok : n_tok + n_wt]
    before = None if own_half else refs[n_tok + n_wt]
    out, xbuf, wbuf, acc, xsem, wsem, asem = refs[n_tok + n_wt + (0 if own_half else 1) :]
    x, _, y, _, _ = position()
    blocks = [2 * k + (y // 2 if own_half else 1 - y // 2) for k in range(2)]
    wanted = [block != lax.rem(x + 2, 4) for block in blocks]
    if not own_half:
        load = pltpu.make_async_copy(before, acc, asem)
        load.start()
    for k in range(2):

        @pl.when(wanted[k])
        def _(k=k):
            start_weights(blocks[k], wbuf.at[k], weights, weight_spots, wsem.at[k])

        for j in range(3):

            @pl.when(blocks[k] == lax.rem(x + STEPS[j] + 4, 4))
            def _(k=k, j=j):
                start_tokens(xbuf.at[k], tokens, token_spots[j], xsem.at[k])

    if not own_half:
        load.wait()
    else:

        @pl.when(jnp.logical_not(wanted[0]))
        def _():
            acc[...] = jnp.zeros_like(acc)

    for k in range(2):

        @pl.when(wanted[k])
        def _(k=k):
            wait_all(xbuf.at[k], xsem.at[k])
            wait_all(wbuf.at[k], wsem.at[k])

            @pl.loop(0, acc.shape[0] // TILE)
            def _(i):
                here = pl.ds(pl.multiple_of(i * TILE, TILE), TILE)
                part = jnp.dot(xbuf[k, here], wbuf[k], preferred_element_type=jnp.float32)
                if k == 0 and own_half:
                    acc[here] = part
                else:
                    acc[here] += part

    store = pltpu.make_async_copy(acc, out, asem)
    store.start()
    store.wait()


def product(own_half, before, tokens, token_spots, weights, weight_spots, rows, depth, name):
    width = weights[0].shape[-1]
    operands = [*tokens, *weights] + ([] if own_half else [before])
    return pl.pallas_call(
        functools.partial(product_kernel, own_half, len(tokens), len(weights), token_spots, weight_spots),
        out_shape=jax.ShapeDtypeStruct((rows, width), jnp.float32),
        in_specs=[HBM] * len(operands),
        out_specs=HBM,
        scratch_shapes=[
            pltpu.VMEM((2, rows, depth), jnp.bfloat16),
            pltpu.VMEM((2, depth, width), jnp.bfloat16),
            pltpu.VMEM((rows, width), jnp.float32),
            pltpu.SemaphoreType.DMA((2,)),
            pltpu.SemaphoreType.DMA((2,)),
            pltpu.SemaphoreType.DMA,
        ],
        compiler_params=pltpu.CompilerParams(vmem_limit_bytes=SCOPED),
        cost_estimate=FREE,
        name=name,
    )(*operands)


def finish_kernel(n_tok, n_wt, token_spots, weight_spots, *refs):
    tokens, weights = refs[:n_tok], refs[n_tok : n_tok + n_wt]
    inv, before, out, xbuf, wbuf, acc, xsem, wsem, asem = refs[n_tok + n_wt :]
    x = position()[0]
    start_weights(lax.rem(x + 2, 4), wbuf, weights, weight_spots, wsem)
    tiles = acc.shape[0] // TILE
    loads = []
    for i in range(tiles):
        spots = []
        for which, row, side, first, size in token_spots:
            low, high = max(row, i * TILE), min(row + size, (i + 1) * TILE)
            if low < high:
                spots.append((which, low, side, first + low - row, high - low))
        start_tokens(xbuf, tokens, spots, xsem.at[i])
        here = pl.ds(i * TILE, TILE)
        loads.append(pltpu.make_async_copy(before.at[here], acc.at[here], asem.at[i]))
        loads[i].start()
    wait_all(wbuf, wsem)
    for i in range(tiles):
        here = pl.ds(i * TILE, TILE)
        wait_all(xbuf.at[here], xsem.at[i])
        loads[i].wait()
        part = jnp.dot(xbuf[here], wbuf[...], preferred_element_type=jnp.float32)
        out[here] = silu((acc[here] + part) * inv[here]).astype(out.dtype)


def finish(tokens, token_spots, weights, weight_spots, inv, before, depth):
    rows, width = before.shape
    return pl.pallas_call(
        functools.partial(finish_kernel, len(tokens), len(weights), token_spots, weight_spots),
        out_shape=jax.ShapeDtypeStruct((rows, width), jnp.bfloat16),
        in_specs=[HBM] * (len(tokens) + len(weights)) + [VMEM, HBM],
        out_specs=VMEM,
        scratch_shapes=[
            pltpu.VMEM((rows, depth), jnp.bfloat16),
            pltpu.VMEM((depth, width), jnp.bfloat16),
            pltpu.VMEM((rows, width), jnp.float32),
            pltpu.SemaphoreType.DMA((rows // TILE,)),
            pltpu.SemaphoreType.DMA,
            pltpu.SemaphoreType.DMA((rows // TILE,)),
        ],
        compiler_params=pltpu.CompilerParams(vmem_limit_bytes=SCOPED),
        cost_estimate=FREE,
        name="product_rest",
    )(*tokens, *weights, inv, before)


def packed(square, columns):
    lead = lax.reduce_precision(square, 8, 7)
    fill = jnp.zeros((2 * columns - square.shape[0],), jnp.float32)
    flat = jnp.concatenate([lead, fill, square - lead, fill]).reshape(4, columns)
    return jnp.concatenate([flat, jnp.zeros((12, columns), jnp.float32)], axis=0).astype(jnp.bfloat16)


def local(tokens, gain, rollout_weight, delta_values, scale_exponents):
    count, features = tokens.shape
    total = features * 8
    block, width = rollout_weight.shape[0] // 16, rollout_weight.shape[1]
    base = rollout_weight.reshape(128, block // 8, width)
    n_a, n_b, n_c = 3 * count // 8, 3 * count // 8, count // 4
    at_b, at_c, extra = n_a, n_a + n_b, 16
    depth = 2 * features

    parts = scaled_delta(scale_exponents, delta_values)
    got = [parts[0]] + [shift(parts[j], x=j) for j in (1, 2, 3)]
    values = tokens.astype(jnp.float32)
    scaled = (values * gain[None, :]).astype(jnp.bfloat16)
    square = jnp.sum(values * values, axis=1)
    mine_a = jnp.concatenate([scaled[:n_a], packed(square, features)], axis=0)
    mine_b, mine_c = scaled[at_b:at_c], scaled[at_c:]
    mine_a, *_ = gate(mine_a, *parts)
    theirs_a = shift(mine_a, z_lo=1)

    got[1], got[2], got[3], mine_c = gate(got[1], got[2], got[3], mine_c)
    same = jnp.stack([g[0] for g in got])
    other = jnp.stack([g[1] for g in got])
    near, across = shift(other, z_lo=1), shift(other, z_lo=1, z_hi=1)
    left_c, right_c = shift(mine_c, x=1), shift(mine_c, x=-1)

    pair_a = jnp.concatenate([mine_a, theirs_a], axis=0)
    near, across, left_c, right_c, same_z, pair_a = gate(near, across, left_c, right_c, same, pair_a)
    left_a, right_a = shift(pair_a, x=1), shift(pair_a, x=-1)
    far = shift(same_z, z_hi=1)
    own = refresh(same, near, base, 0, "refresh_own")
    own_pair = [own, shift(own, core=1)]
    own_next = [shift(v, y_by_core=1) for v in own_pair]
    mine_bz, far = gate(mine_b, far)
    theirs_b = shift(mine_bz, z_lo=1)
    other_hi = refresh(far, across, base, 1, "refresh_far")
    far_pair = jnp.stack([other_hi, shift(other_hi, core=1)])

    left_a, right_a, *own_next, theirs_b = gate(left_a, right_a, *own_next, theirs_b)
    pair_b = jnp.concatenate([mine_b, theirs_b], axis=0)
    left_b, right_b = shift(pair_b, x=1), shift(pair_b, x=-1)
    far_next = shift(far_pair, y_by_core=1)
    own_opp = shift(own_next[0], y_by_core=1)
    theirs_c = shift(jnp.concatenate([mine_c, left_c, right_c], axis=0), z_lo=1)

    left_b, right_b, far_next, theirs_c, own_opp, *own_next = gate(
        left_b, right_b, far_next, theirs_c, own_opp, *own_next
    )
    up = shift(jnp.concatenate([left_a, theirs_c[n_c : 2 * n_c]], axis=0), x=1)
    down = shift(jnp.concatenate([right_b, right_c], axis=0), x=-1)
    far_opp = shift(far_next[0], y_by_core=1)
    far_swap = shift(far_next, core=1)
    own_swap = [shift(v, core=1) for v in own_next]

    tokens_all = [pair_a, left_a, right_a, pair_b, left_b, right_b, mine_c, left_c, right_c, theirs_c]
    token_spots = []
    for j in range(3):
        spots = [(j, 0, side, side * (n_a + extra), n_a) for side in (0, 1)]
        spots += [(3 + j, at_b, side, side * n_b, n_b) for side in (0, 1)]
        token_spots.append(spots + [(6 + j, at_c, 0, 0, n_c), (9, at_c, 1, j * n_c, n_c)])
    weights = [*own_pair, *own_next, *own_swap, far_pair, far_next, far_swap]
    weight_spots = []
    for k, (step, cores) in enumerate(((0, (0, 1)), (-1, (0, 1)), (1, (1, 0)))):
        for index in (0, 1):
            weight_spots.append((2 * k + index, None, step, cores[index], 0))
            weight_spots.append((6 + k, index, step, cores[index], 1))
    partial = product(True, None, tokens_all, token_spots, weights, weight_spots, count, depth, "product_own_half")

    own_opp, far_opp, partial, far_swap, *own_swap = gate(own_opp, far_opp, partial, far_swap, *own_swap)
    weights = [*own_pair, *own_next, *own_swap, far_pair, far_next, far_swap]
    weights += [own_opp, shift(own_opp, core=1), far_opp, shift(far_opp, core=1)]
    weight_spots += [(9 + 2 * hi + c, None, 2, c, hi) for hi in (0, 1) for c in (0, 1)]
    partial = product(
        False, partial, tokens_all, token_spots, weights, weight_spots, count, depth, "product_other_half"
    )

    partial, up = gate(partial, up)
    tail = sum(
        v[at : at + 4].astype(jnp.float32)
        for v in (pair_a, left_a, right_a, up)
        for at in (n_a, 2 * n_a + extra)
    ).reshape(2, 2 * features)
    inv = lax.rsqrt((tail[0] + tail[1])[:count] / total + 1e-06)[:, None]
    spots = [(0, 0, side, side * (n_a + extra), n_a) for side in (0, 1)]
    spots += [(1, at_b, side, side * n_b, n_b) for side in (0, 1)]
    spots += [(1, at_c, 0, 2 * n_b, n_c), (0, at_c, 1, 2 * (n_a + extra), n_c)]
    return finish([up, down], spots, weights, weight_spots, inv, partial, depth)


def solution(mesh):
    in_specs = (
        P("fsdp", "tp"),
        P("tp"),
        P(None, "tp"),
        P(("fsdp", "tp"), None),
        P(("fsdp", "tp"), None),
    )
    out_specs = P("fsdp", "tp")
    return jax.shard_map(local, mesh=mesh, in_specs=in_specs, out_specs=out_specs, check_vma=False)
```

```python
import functools

import jax
import jax.numpy as jnp
from jax import lax
from jax.experimental import pallas as pl
from jax.experimental.pallas import tpu as pltpu
from jax.sharding import PartitionSpec as P


SCOPED = 60 * 2**20
FREE = pl.CostEstimate(flops=0, bytes_accessed=0, transcendentals=0)


def links(x=0, z_lo=0, z_hi=0, y=0, core=0):
    pairs = []
    for f in range(16):
        for t in range(8):
            f2 = (((f // 8) + z_hi) % 2) * 8 + (((f // 2) % 4 + y) % 4) * 2 + (f + core) % 2
            t2 = ((t // 2 + x) % 4) * 2 + (t + z_lo) % 2
            pairs.append((f * 8 + t, f2 * 8 + t2))
    return pairs


def shift(value, **step):
    return lax.ppermute(value, ("fsdp", "tp"), links(**step))


def position():
    f, t = lax.axis_index("fsdp"), lax.axis_index("tp")
    return t // 2, t % 2, (f // 2) % 4, f // 8, f % 2


def power_two(exps):
    total = jnp.zeros(exps.shape, jnp.float32)
    for level in range(-8, -4):
        total = total + jnp.where(exps == level, jnp.float32(2.0**level), jnp.float32(0.0))
    return total


def scale_kernel(exps, delta, *outs):
    groups = exps.shape[1]
    scale = power_two(exps[...])
    x, z_lo, _, _, _ = position()
    width = outs[0].shape[2]
    per = width // 128
    scaled = []
    for owner in range(8):
        columns = []
        for g in range(per):
            at = owner * per + g
            piece = delta[:, at * 128 : (at + 1) * 128].astype(jnp.float32) * scale[:, at : at + 1]
            columns.append(piece.astype(jnp.bfloat16))
        block = jnp.concatenate(columns, axis=1)
        j = lax.rem(owner // 2 - x + 4, 4)
        half = jnp.where(z_lo == owner % 2, 0, 1)
        for k in range(4):
            @pl.when(j == k)
            def _(k=k, block=block, half=half):
                outs[k][half] = block


def scaled_delta(exps, delta):
    rows, wide = delta.shape
    width = wide // 8
    return pl.pallas_call(
        scale_kernel,
        out_shape=[jax.ShapeDtypeStruct((2, rows, width), jnp.bfloat16)] * 4,
        in_specs=[pl.BlockSpec(memory_space=pltpu.VMEM)] * 2,
        out_specs=[pl.BlockSpec(memory_space=pltpu.VMEM)] * 4,
        compiler_params=pltpu.CompilerParams(vmem_limit_bytes=SCOPED),
        cost_estimate=FREE,
        name="scaled_delta",
    )(exps, delta)


def refresh_kernel(other_hi, same, other, base, out, held, sem):
    x, z_lo, y, z_hi, core = position()
    owner = lax.rem(z_hi + other_hi, 2) * 8 + y * 2 + core
    copy = pltpu.make_async_copy(base.at[pl.ds(owner * 8, 8)], held, sem)
    copy.start()
    copy.wait()
    for t in range(8):
        j = lax.rem(x - t // 2 + 4, 4)
        delta = jnp.where(z_lo == t % 2, same[j].astype(jnp.float32), other[j].astype(jnp.float32))
        out[t] = (held[t].astype(jnp.float32) + delta).astype(jnp.bfloat16)


def refresh(same, other, base, other_hi, name):
    shape = (8, *base.shape[1:])
    vmem = pl.BlockSpec(memory_space=pltpu.VMEM)
    out = pl.pallas_call(
        functools.partial(refresh_kernel, other_hi),
        out_shape=jax.ShapeDtypeStruct(shape, jnp.bfloat16),
        in_specs=[vmem, vmem, pl.BlockSpec(memory_space=pltpu.HBM)],
        out_specs=vmem,
        scratch_shapes=[pltpu.VMEM(shape, jnp.bfloat16), pltpu.SemaphoreType.DMA],
        compiler_params=pltpu.CompilerParams(vmem_limit_bytes=SCOPED),
        cost_estimate=FREE,
        name=name,
    )(same, other, base)
    return out.reshape(8 * shape[1], shape[2])


def gate(*values):
    return lax.optimization_barrier(values)


STEPS = (0, -1, 1, 2)
TILE = 256
HBM = pl.BlockSpec(memory_space=pltpu.HBM)
VMEM = pl.BlockSpec(memory_space=pltpu.VMEM)


def silu(hidden):
    return hidden / (1.0 + jnp.exp(-hidden))


def start_weights(block, held, pieces, spots, sem):
    _, _, y, z_hi, core = position()
    piece = held.shape[0] // 4
    for which, step, other_core, other_hi in spots:
        y2 = lax.rem(y + step + 4, 4)
        part = lax.rem(y2, 2) * 2 + lax.rem(core + other_core, 2)

        @pl.when(lax.rem(z_hi + other_hi, 2) * 2 + y2 // 2 == block)
        def _(which=which, part=part):
            target = held.at[pl.ds(pl.multiple_of(part * piece, 16), piece)]
            pltpu.make_async_copy(pieces[which], target, sem).start()


def start_tokens(held, pieces, spots, sem):
    z_lo = position()[1]
    half = held.shape[1] // 2
    for which, row, side, first, size in spots:
        column = jnp.where(z_lo == 0, side, 1 - side)
        target = held.at[pl.ds(row, size), pl.ds(pl.multiple_of(column * half, 128), half)]
        pltpu.make_async_copy(pieces[which].at[pl.ds(first, size)], target, sem).start()


def wait_all(held, sem):
    pltpu.make_async_copy(held, held, sem).wait()


def product_kernel(n_tok, n_wt, token_spots, weight_spots, *refs):
    tokens, weights = refs[:n_tok], refs[n_tok : n_tok + n_wt]
    out, xbuf, wbuf, acc, xsem, wsem, asem = refs[n_tok + n_wt :]
    x = position()[0]

    def start(j):
        start_weights(lax.rem(x + STEPS[j] + 4, 4), wbuf.at[j], weights, weight_spots, wsem.at[j])
        start_tokens(xbuf.at[j], tokens, token_spots[j], xsem.at[j])

    start(0)
    for j in range(3):
        wait_all(xbuf.at[j], xsem.at[j])
        wait_all(wbuf.at[j], wsem.at[j])
        if j < 2:
            start(j + 1)

        @pl.loop(0, acc.shape[0] // TILE)
        def _(i, j=j):
            here = pl.ds(pl.multiple_of(i * TILE, TILE), TILE)
            part = jnp.dot(xbuf[j, here], wbuf[j], preferred_element_type=jnp.float32)
            if j == 0:
                acc[here] = part
            else:
                acc[here] += part

    store = pltpu.make_async_copy(acc, out, asem)
    store.start()
    store.wait()


def product(tokens, token_spots, weights, weight_spots, rows, depth):
    width = weights[0].shape[-1]
    operands = [*tokens, *weights]
    return pl.pallas_call(
        functools.partial(product_kernel, len(tokens), len(weights), token_spots, weight_spots),
        out_shape=jax.ShapeDtypeStruct((rows, width), jnp.float32),
        in_specs=[HBM] * len(operands),
        out_specs=HBM,
        scratch_shapes=[
            pltpu.VMEM((3, rows, depth), jnp.bfloat16),
            pltpu.VMEM((3, depth, width), jnp.bfloat16),
            pltpu.VMEM((rows, width), jnp.float32),
            pltpu.SemaphoreType.DMA((3,)),
            pltpu.SemaphoreType.DMA((3,)),
            pltpu.SemaphoreType.DMA,
        ],
        compiler_params=pltpu.CompilerParams(vmem_limit_bytes=SCOPED),
        cost_estimate=FREE,
        name="product_most",
    )(*operands)


def finish_kernel(n_tok, n_wt, token_spots, weight_spots, *refs):
    tokens, weights = refs[:n_tok], refs[n_tok : n_tok + n_wt]
    inv, before, out, xbuf, wbuf, acc, xsem, wsem, asem = refs[n_tok + n_wt :]
    x = position()[0]
    start_weights(lax.rem(x + 2, 4), wbuf, weights, weight_spots, wsem)
    tiles = acc.shape[0] // TILE
    loads = []
    for i in range(tiles):
        spots = []
        for which, row, side, first, size in token_spots:
            low, high = max(row, i * TILE), min(row + size, (i + 1) * TILE)
            if low < high:
                spots.append((which, low, side, first + low - row, high - low))
        start_tokens(xbuf, tokens, spots, xsem.at[i])
        here = pl.ds(i * TILE, TILE)
        loads.append(pltpu.make_async_copy(before.at[here], acc.at[here], asem.at[i]))
        loads[i].start()
    wait_all(wbuf, wsem)
    for i in range(tiles):
        here = pl.ds(i * TILE, TILE)
        wait_all(xbuf.at[here], xsem.at[i])
        loads[i].wait()
        part = jnp.dot(xbuf[here], wbuf[...], preferred_element_type=jnp.float32)
        out[here] = silu((acc[here] + part) * inv[here]).astype(out.dtype)


def finish(tokens, token_spots, weights, weight_spots, inv, before, depth):
    rows, width = before.shape
    return pl.pallas_call(
        functools.partial(finish_kernel, len(tokens), len(weights), token_spots, weight_spots),
        out_shape=jax.ShapeDtypeStruct((rows, width), jnp.bfloat16),
        in_specs=[HBM] * (len(tokens) + len(weights)) + [VMEM, HBM],
        out_specs=VMEM,
        scratch_shapes=[
            pltpu.VMEM((rows, depth), jnp.bfloat16),
            pltpu.VMEM((depth, width), jnp.bfloat16),
            pltpu.VMEM((rows, width), jnp.float32),
            pltpu.SemaphoreType.DMA((rows // TILE,)),
            pltpu.SemaphoreType.DMA,
            pltpu.SemaphoreType.DMA((rows // TILE,)),
        ],
        compiler_params=pltpu.CompilerParams(vmem_limit_bytes=SCOPED),
        cost_estimate=FREE,
        name="product_rest",
    )(*tokens, *weights, inv, before)


def packed(square, columns):
    lead = lax.reduce_precision(square, 8, 7)
    fill = jnp.zeros((2 * columns - square.shape[0],), jnp.float32)
    flat = jnp.concatenate([lead, fill, square - lead, fill]).reshape(4, columns)
    return jnp.concatenate([flat, jnp.zeros((12, columns), jnp.float32)], axis=0).astype(jnp.bfloat16)


def local(tokens, gain, rollout_weight, delta_values, scale_exponents):
    count, features = tokens.shape
    total = features * 8
    block, width = rollout_weight.shape[0] // 16, rollout_weight.shape[1]
    base = rollout_weight.reshape(128, block // 8, width)
    n_a, n_b, n_c = count // 4, 7 * count // 16, 5 * count // 16
    at_b, at_c, extra = n_a, n_a + n_b, 16
    depth = 2 * features

    parts = scaled_delta(scale_exponents, delta_values)
    got = [parts[0]] + [shift(parts[j], x=j) for j in (1, 2, 3)]
    values = tokens.astype(jnp.float32)
    scaled = (values * gain[None, :]).astype(jnp.bfloat16)
    square = jnp.sum(values * values, axis=1)
    mine_a = jnp.concatenate([scaled[:n_a], packed(square, features)], axis=0)
    mine_b, mine_c = scaled[at_b:at_c], scaled[at_c:]
    mine_a, *_ = gate(mine_a, *parts)
    theirs_a = shift(mine_a, z_lo=1)

    got[1], got[2], got[3], mine_c = gate(got[1], got[2], got[3], mine_c)
    same = jnp.stack([g[0] for g in got])
    other = jnp.stack([g[1] for g in got])
    near, across = shift(other, z_lo=1), shift(other, z_lo=1, z_hi=1)
    left_c, right_c = shift(mine_c, x=1), shift(mine_c, x=-1)

    pair_a = jnp.concatenate([mine_a, theirs_a], axis=0)
    near, across, left_c, right_c, same_z, pair_a = gate(near, across, left_c, right_c, same, pair_a)
    left_a, right_a = shift(pair_a, x=1), shift(pair_a, x=-1)
    far = shift(same_z, z_hi=1)
    own = refresh(same, near, base, 0, "refresh_own")
    own_l, own_r = shift(own, y=1), shift(own, y=-1)
    mine_bz, far = gate(mine_b, far)
    theirs_b = shift(mine_bz, z_lo=1)
    other_hi = refresh(far, across, base, 1, "refresh_far")

    left_a, right_a, own_l, own_r, right_c = gate(left_a, right_a, own_l, own_r, right_c)
    opposite_a, opposite_c = shift(left_a, x=1), shift(right_c, x=-1)
    far_l, far_r = shift(other_hi, y=1), shift(other_hi, y=-1)
    pair_b = jnp.concatenate([mine_b, theirs_b], axis=0)
    left_b, right_b = shift(pair_b, x=1), shift(pair_b, x=-1)
    three_c, theirs_b = gate(jnp.concatenate([mine_c, left_c, right_c], axis=0), theirs_b)
    theirs_c = shift(three_c, z_lo=1)
    own_lf, far_l, far_r = gate(own_l, far_l, far_r)
    own_o, far_o = shift(own_lf, y=1), shift(far_r, y=-1)
    rings = [own, own_l, own_r, other_hi, far_l, far_r]
    swaps = [shift(v, core=1) for v in rings]

    left_b, right_b, theirs_c, own_o, far_o, opposite_a, opposite_c = gate(
        left_b, right_b, theirs_c, own_o, far_o, opposite_a, opposite_c
    )
    cut = (2 * n_b - n_c) // 32 * 16
    up = shift(jnp.concatenate([theirs_c[n_c : 2 * n_c], left_b[:cut]], axis=0), x=1)
    down = shift(right_b[cut:], x=-1)

    tokens_all = [pair_a, left_a, right_a, pair_b, left_b, right_b, mine_c, left_c, right_c, theirs_c]
    token_spots = []
    for j in range(3):
        spots = [(j, 0, side, side * (n_a + extra), n_a) for side in (0, 1)]
        spots += [(3 + j, at_b, side, side * n_b, n_b) for side in (0, 1)]
        token_spots.append(spots + [(6 + j, at_c, 0, 0, n_c), (9, at_c, 1, j * n_c, n_c)])
    weights = [*rings, *swaps, own_o, far_o, shift(own_o, core=1), shift(far_o, core=1)]
    weight_spots = [(6 * c + 3 * hi + k, STEPS[k], c, hi) for c in (0, 1) for hi in (0, 1) for k in range(3)]
    weight_spots += [(12 + 2 * c + hi, 2, c, hi) for c in (0, 1) for hi in (0, 1)]
    partial = product(tokens_all, token_spots, weights, weight_spots, count, depth)

    tail = sum(
        v[at : at + 4].astype(jnp.float32)
        for v in (pair_a, left_a, right_a, opposite_a)
        for at in (n_a, 2 * n_a + extra)
    ).reshape(2, 2 * features)
    inv = lax.rsqrt((tail[0] + tail[1])[:count] / total + 1e-06)[:, None]
    spots = [(0, 0, side, side * (n_a + extra), n_a) for side in (0, 1)]
    spots += [(1, at_c, 0, 0, n_c), (2, at_c, 1, 0, n_c)]
    spots += [(2, at_b, 0, n_c, cut), (3, at_b + cut, 0, 0, n_b - cut), (3, at_b, 1, n_b - cut, n_b)]
    return finish([opposite_a, opposite_c, up, down], spots, weights, weight_spots, inv, partial, depth)


def solution(mesh):
    in_specs = (
        P("fsdp", "tp"),
        P("tp"),
        P(None, "tp"),
        P(("fsdp", "tp"), None),
        P(("fsdp", "tp"), None),
    )
    out_specs = P("fsdp", "tp")
    return jax.shard_map(local, mesh=mesh, in_specs=in_specs, out_specs=out_specs, check_vma=False)
```

```python
import functools

import jax
import jax.numpy as jnp
from jax import lax
from jax.experimental import pallas as pl
from jax.experimental.pallas import tpu as pltpu
from jax.sharding import PartitionSpec as P


SCOPED = 60 * 2**20
FREE = pl.CostEstimate(flops=0, bytes_accessed=0, transcendentals=0)


def links(x=0, z_lo=0, z_hi=0, y=0, core=0):
    pairs = []
    for f in range(16):
        for t in range(8):
            f2 = (((f // 8) + z_hi) % 2) * 8 + (((f // 2) % 4 + y) % 4) * 2 + (f + core) % 2
            t2 = ((t // 2 + x) % 4) * 2 + (t + z_lo) % 2
            pairs.append((f * 8 + t, f2 * 8 + t2))
    return pairs


def shift(value, **step):
    return lax.ppermute(value, ("fsdp", "tp"), links(**step))


def position():
    f, t = lax.axis_index("fsdp"), lax.axis_index("tp")
    return t // 2, t % 2, (f // 2) % 4, f // 8, f % 2


def power_two(exps):
    total = jnp.zeros(exps.shape, jnp.float32)
    for level in range(-8, -4):
        total = total + jnp.where(exps == level, jnp.float32(2.0**level), jnp.float32(0.0))
    return total


def scale_kernel(exps, delta, *refs):
    outs, held, sems = refs[:4], refs[4], refs[5]
    scale = power_two(exps[...])
    x, z_lo, _, _, _ = position()
    width = held.shape[2]
    for g in range(exps.shape[1]):
        piece = delta[:, g * 128 : (g + 1) * 128].astype(jnp.float32) * scale[:, g : g + 1]
        owner, at = divmod(g * 128, width)
        held[owner, :, at : at + 128] = piece.astype(jnp.bfloat16)
    copies = []
    for j in range(4):
        for half in (0, 1):
            owner = lax.rem(x + j, 4) * 2 + (z_lo if half == 0 else 1 - z_lo)
            copies.append(pltpu.make_async_copy(held.at[owner], outs[j].at[half], sems.at[2 * j + half]))
            copies[-1].start()
    for copy in copies:
        copy.wait()


def scaled_delta(exps, delta):
    rows, wide = delta.shape
    width = wide // 8
    return pl.pallas_call(
        scale_kernel,
        out_shape=[jax.ShapeDtypeStruct((2, rows, width), jnp.bfloat16)] * 4,
        in_specs=[pl.BlockSpec(memory_space=pltpu.VMEM)] * 2,
        out_specs=[pl.BlockSpec(memory_space=pltpu.HBM)] * 4,
        scratch_shapes=[pltpu.VMEM((8, rows, width), jnp.bfloat16), pltpu.SemaphoreType.DMA((8,))],
        compiler_params=pltpu.CompilerParams(vmem_limit_bytes=SCOPED),
        cost_estimate=FREE,
        name="scaled_delta",
    )(exps, delta)


def refresh_kernel(other_hi, same, other, base, out, held, sem):
    x, z_lo, y, z_hi, core = position()
    owner = lax.rem(z_hi + other_hi, 2) * 8 + y * 2 + core
    copy = pltpu.make_async_copy(base.at[pl.ds(owner * 8, 8)], held, sem)
    copy.start()
    copy.wait()
    for t in range(8):
        j = lax.rem(x - t // 2 + 4, 4)
        delta = jnp.where(z_lo == t % 2, same[j].astype(jnp.float32), other[j].astype(jnp.float32))
        out[t] = (held[t].astype(jnp.float32) + delta).astype(jnp.bfloat16)


def refresh(same, other, base, other_hi, name):
    shape = (8, *base.shape[1:])
    vmem = pl.BlockSpec(memory_space=pltpu.VMEM)
    out = pl.pallas_call(
        functools.partial(refresh_kernel, other_hi),
        out_shape=jax.ShapeDtypeStruct(shape, jnp.bfloat16),
        in_specs=[vmem, vmem, pl.BlockSpec(memory_space=pltpu.HBM)],
        out_specs=vmem,
        scratch_shapes=[pltpu.VMEM(shape, jnp.bfloat16), pltpu.SemaphoreType.DMA],
        compiler_params=pltpu.CompilerParams(vmem_limit_bytes=SCOPED),
        cost_estimate=FREE,
        name=name,
    )(same, other, base)
    return out.reshape(8 * shape[1], shape[2])


def gate(*values):
    return lax.optimization_barrier(values)


STEPS = (0, -1, 1, 2)
TILE = 256
HBM = pl.BlockSpec(memory_space=pltpu.HBM)
VMEM = pl.BlockSpec(memory_space=pltpu.VMEM)


def silu(hidden):
    return hidden / (1.0 + jnp.exp(-hidden))


def start_weights(block, held, pieces, spots, sem):
    _, _, y, z_hi, core = position()
    piece = held.shape[0] // 4
    for which, step, other_core, other_hi in spots:
        y2 = lax.rem(y + step + 4, 4)
        part = lax.rem(y2, 2) * 2 + lax.rem(core + other_core, 2)

        @pl.when(lax.rem(z_hi + other_hi, 2) * 2 + y2 // 2 == block)
        def _(which=which, part=part):
            target = held.at[pl.ds(pl.multiple_of(part * piece, 16), piece)]
            pltpu.make_async_copy(pieces[which], target, sem).start()


def start_tokens(held, pieces, spots, sem):
    z_lo = position()[1]
    half = held.shape[1] // 2
    for which, row, side, first, size in spots:
        column = jnp.where(z_lo == 0, side, 1 - side)
        target = held.at[pl.ds(row, size), pl.ds(pl.multiple_of(column * half, 128), half)]
        pltpu.make_async_copy(pieces[which].at[pl.ds(first, size)], target, sem).start()


def wait_all(held, sem):
    pltpu.make_async_copy(held, held, sem).wait()


def product_kernel(n_tok, n_wt, token_spots, weight_spots, *refs):
    tokens, weights = refs[:n_tok], refs[n_tok : n_tok + n_wt]
    out, xbuf, wbuf, acc, xsem, wsem, asem = refs[n_tok + n_wt :]
    x = position()[0]

    def start(j):
        start_weights(lax.rem(x + STEPS[j] + 4, 4), wbuf.at[j], weights, weight_spots, wsem.at[j])
        start_tokens(xbuf.at[j], tokens, token_spots[j], xsem.at[j])

    start(0)
    for j in range(3):
        wait_all(xbuf.at[j], xsem.at[j])
        wait_all(wbuf.at[j], wsem.at[j])
        if j < 2:
            start(j + 1)

        @pl.loop(0, acc.shape[0] // TILE)
        def _(i, j=j):
            here = pl.ds(pl.multiple_of(i * TILE, TILE), TILE)
            part = jnp.dot(xbuf[j, here], wbuf[j], preferred_element_type=jnp.float32)
            if j == 0:
                acc[here] = part
            else:
                acc[here] += part

    store = pltpu.make_async_copy(acc, out, asem)
    store.start()
    store.wait()


def product(tokens, token_spots, weights, weight_spots, rows, depth):
    width = weights[0].shape[-1]
    operands = [*tokens, *weights]
    return pl.pallas_call(
        functools.partial(product_kernel, len(tokens), len(weights), token_spots, weight_spots),
        out_shape=jax.ShapeDtypeStruct((rows, width), jnp.float32),
        in_specs=[HBM] * len(operands),
        out_specs=HBM,
        scratch_shapes=[
            pltpu.VMEM((3, rows, depth), jnp.bfloat16),
            pltpu.VMEM((3, depth, width), jnp.bfloat16),
            pltpu.VMEM((rows, width), jnp.float32),
            pltpu.SemaphoreType.DMA((3,)),
            pltpu.SemaphoreType.DMA((3,)),
            pltpu.SemaphoreType.DMA,
        ],
        compiler_params=pltpu.CompilerParams(vmem_limit_bytes=SCOPED),
        cost_estimate=FREE,
        name="product_most",
    )(*operands)


def finish_kernel(n_tok, n_wt, token_spots, weight_spots, *refs):
    tokens, weights = refs[:n_tok], refs[n_tok : n_tok + n_wt]
    inv, before, out, xbuf, wbuf, acc, result, xsem, wsem, asem, osem = refs[n_tok + n_wt :]
    x = position()[0]
    start_weights(lax.rem(x + 2, 4), wbuf, weights, weight_spots, wsem)
    tiles = acc.shape[0] // TILE
    loads = []
    for i in range(tiles):
        spots = []
        for which, row, side, first, size in token_spots:
            low, high = max(row, i * TILE), min(row + size, (i + 1) * TILE)
            if low < high:
                spots.append((which, low, side, first + low - row, high - low))
        start_tokens(xbuf, tokens, spots, xsem.at[i])
        here = pl.ds(i * TILE, TILE)
        loads.append(pltpu.make_async_copy(before.at[here], acc.at[here], asem.at[i]))
        loads[i].start()
    wait_all(wbuf, wsem)
    stores = []
    for i in range(tiles):
        here = pl.ds(i * TILE, TILE)
        wait_all(xbuf.at[here], xsem.at[i])
        loads[i].wait()
        part = jnp.dot(xbuf[here], wbuf[...], preferred_element_type=jnp.float32)
        result[here] = silu((acc[here] + part) * inv[here]).astype(out.dtype)
        stores.append(pltpu.make_async_copy(result.at[here], out.at[here], osem.at[i]))
        stores[i].start()
    for store in stores:
        store.wait()


def finish(tokens, token_spots, weights, weight_spots, inv, before, depth):
    rows, width = before.shape
    return pl.pallas_call(
        functools.partial(finish_kernel, len(tokens), len(weights), token_spots, weight_spots),
        out_shape=jax.ShapeDtypeStruct((rows, width), jnp.bfloat16),
        in_specs=[HBM] * (len(tokens) + len(weights)) + [VMEM, HBM],
        out_specs=HBM,
        scratch_shapes=[
            pltpu.VMEM((rows, depth), jnp.bfloat16),
            pltpu.VMEM((depth, width), jnp.bfloat16),
            pltpu.VMEM((rows, width), jnp.float32),
            pltpu.VMEM((rows, width), jnp.bfloat16),
            pltpu.SemaphoreType.DMA((rows // TILE,)),
            pltpu.SemaphoreType.DMA,
            pltpu.SemaphoreType.DMA((rows // TILE,)),
            pltpu.SemaphoreType.DMA((rows // TILE,)),
        ],
        compiler_params=pltpu.CompilerParams(vmem_limit_bytes=SCOPED),
        cost_estimate=FREE,
        name="product_rest",
    )(*tokens, *weights, inv, before)


def packed(square, columns):
    lead = lax.reduce_precision(square, 8, 7)
    fill = jnp.zeros((2 * columns - square.shape[0],), jnp.float32)
    flat = jnp.concatenate([lead, fill, square - lead, fill]).reshape(4, columns)
    return jnp.concatenate([flat, jnp.zeros((12, columns), jnp.float32)], axis=0).astype(jnp.bfloat16)


def local(tokens, gain, rollout_weight, delta_values, scale_exponents):
    count, features = tokens.shape
    total = features * 8
    block, width = rollout_weight.shape[0] // 16, rollout_weight.shape[1]
    base = rollout_weight.reshape(128, block // 8, width)
    n_a, n_b, n_c = count // 4, 7 * count // 16, 5 * count // 16
    at_b, at_c, extra = n_a, n_a + n_b, 16
    depth = 2 * features

    parts = scaled_delta(scale_exponents, delta_values)
    got = [parts[0]] + [shift(parts[j], x=j) for j in (1, 2, 3)]
    values = tokens.astype(jnp.float32)
    scaled = (values * gain[None, :]).astype(jnp.bfloat16)
    square = jnp.sum(values * values, axis=1)
    mine_a = jnp.concatenate([scaled[:n_a], packed(square, features)], axis=0)
    mine_b, mine_c = scaled[at_b:at_c], scaled[at_c:]
    mine_a, *_ = gate(mine_a, *parts)
    theirs_a = shift(mine_a, z_lo=1)

    got[1], got[2], got[3], mine_c = gate(got[1], got[2], got[3], mine_c)
    same = jnp.stack([g[0] for g in got])
    other = jnp.stack([g[1] for g in got])
    near, across = shift(other, z_lo=1), shift(other, z_lo=1, z_hi=1)
    left_c, right_c = shift(mine_c, x=1), shift(mine_c, x=-1)

    pair_a = jnp.concatenate([mine_a, theirs_a], axis=0)
    near, across, left_c, right_c, same_z, pair_a = gate(near, across, left_c, right_c, same, pair_a)
    left_a, right_a = shift(pair_a, x=1), shift(pair_a, x=-1)
    far = shift(same_z, z_hi=1)
    own = refresh(same, near, base, 0, "refresh_own")
    own_l, own_r = shift(own, y=1), shift(own, y=-1)
    mine_bz, far = gate(mine_b, far)
    theirs_b = shift(mine_bz, z_lo=1)
    other_hi = refresh(far, across, base, 1, "refresh_far")

    left_a, right_a, right_c = gate(left_a, right_a, right_c)
    opposite_a, opposite_c = shift(left_a, x=1), shift(right_c, x=-1)
    other_hi, left_a, right_a, own_l, own_r = gate(other_hi, left_a, right_a, own_l, own_r)
    far_l, far_r = shift(other_hi, y=1), shift(other_hi, y=-1)
    pair_b = jnp.concatenate([mine_b, theirs_b], axis=0)
    pair_b, opposite_a, opposite_c = gate(pair_b, opposite_a, opposite_c)
    left_b, right_b = shift(pair_b, x=1), shift(pair_b, x=-1)
    three_c, theirs_b = gate(jnp.concatenate([mine_c, left_c, right_c], axis=0), theirs_b)
    theirs_c = shift(three_c, z_lo=1)
    own_lf, far_l, far_r = gate(own_l, far_l, far_r)
    own_o, far_o = shift(own_lf, y=1), shift(far_r, y=-1)
    rings = [own, own_l, own_r, other_hi, far_l, far_r]
    swaps = [shift(v, core=1) for v in rings]

    tail = sum(
        v[at : at + 4].astype(jnp.float32)
        for v in (pair_a, left_a, right_a, opposite_a)
        for at in (n_a, 2 * n_a + extra)
    ).reshape(2, 2 * features)
    inv = lax.rsqrt((tail[0] + tail[1])[:count] / total + 1e-06)[:, None]
    left_b, right_b, theirs_c, own_o, far_o, opposite_a, opposite_c, inv = gate(
        left_b, right_b, theirs_c, own_o, far_o, opposite_a, opposite_c, inv
    )
    cut = (2 * n_b - n_c) // 32 * 16
    up = shift(jnp.concatenate([theirs_c[n_c : 2 * n_c], left_b[:cut]], axis=0), x=1)
    down = shift(right_b[cut:], x=-1)

    tokens_all = [pair_a, left_a, right_a, pair_b, left_b, right_b, mine_c, left_c, right_c, theirs_c]
    token_spots = []
    for j in range(3):
        spots = [(j, 0, side, side * (n_a + extra), n_a) for side in (0, 1)]
        spots += [(3 + j, at_b, side, side * n_b, n_b) for side in (0, 1)]
        token_spots.append(spots + [(6 + j, at_c, 0, 0, n_c), (9, at_c, 1, j * n_c, n_c)])
    weights = [*rings, *swaps, own_o, far_o, shift(own_o, core=1), shift(far_o, core=1)]
    weight_spots = [(6 * c + 3 * hi + k, STEPS[k], c, hi) for c in (0, 1) for hi in (0, 1) for k in range(3)]
    weight_spots += [(12 + 2 * c + hi, 2, c, hi) for c in (0, 1) for hi in (0, 1)]
    partial = product(tokens_all, token_spots, weights, weight_spots, count, depth)

    spots = [(0, 0, side, side * (n_a + extra), n_a) for side in (0, 1)]
    spots += [(1, at_c, 0, 0, n_c), (2, at_c, 1, 0, n_c)]
    spots += [(2, at_b, 0, n_c, cut), (3, at_b + cut, 0, 0, n_b - cut), (3, at_b, 1, n_b - cut, n_b)]
    return finish([opposite_a, opposite_c, up, down], spots, weights, weight_spots, inv, partial, depth)


def solution(mesh):
    in_specs = (
        P("fsdp", "tp"),
        P("tp"),
        P(None, "tp"),
        P(("fsdp", "tp"), None),
        P(("fsdp", "tp"), None),
    )
    out_specs = P("fsdp", "tp")
    return jax.shard_map(local, mesh=mesh, in_specs=in_specs, out_specs=out_specs, check_vma=False)
```

```python
import functools

import jax
import jax.numpy as jnp
from jax import lax
from jax.experimental import pallas as pl
from jax.experimental.pallas import tpu as pltpu
from jax.sharding import PartitionSpec as P


SCOPED = 60 * 2**20
FREE = pl.CostEstimate(flops=0, bytes_accessed=0, transcendentals=0)


def links(x=0, z_lo=0, z_hi=0, y=0, core=0):
    pairs = []
    for f in range(16):
        for t in range(8):
            f2 = (((f // 8) + z_hi) % 2) * 8 + (((f // 2) % 4 + y) % 4) * 2 + (f + core) % 2
            t2 = ((t // 2 + x) % 4) * 2 + (t + z_lo) % 2
            pairs.append((f * 8 + t, f2 * 8 + t2))
    return pairs


def shift(value, **step):
    return lax.ppermute(value, ("fsdp", "tp"), links(**step))


def position():
    f, t = lax.axis_index("fsdp"), lax.axis_index("tp")
    return t // 2, t % 2, (f // 2) % 4, f // 8, f % 2


def power_two(exps):
    total = jnp.zeros(exps.shape, jnp.float32)
    for level in range(-8, -4):
        total = total + jnp.where(exps == level, jnp.float32(2.0**level), jnp.float32(0.0))
    return total


def scale_kernel(exps, delta, *refs):
    outs, held, sems = refs[:4], refs[4], refs[5]
    scale = power_two(exps[...])
    x, z_lo, _, _, _ = position()
    width = held.shape[2]
    for g in range(exps.shape[1]):
        piece = delta[:, g * 128 : (g + 1) * 128].astype(jnp.float32) * scale[:, g : g + 1]
        owner, at = divmod(g * 128, width)
        held[owner, :, at : at + 128] = piece.astype(jnp.bfloat16)
    copies = []
    for j in range(4):
        for half in (0, 1):
            owner = lax.rem(x + j, 4) * 2 + (z_lo if half == 0 else 1 - z_lo)
            copies.append(pltpu.make_async_copy(held.at[owner], outs[j].at[half], sems.at[2 * j + half]))
            copies[-1].start()
    for copy in copies:
        copy.wait()


def scaled_delta(exps, delta):
    rows, wide = delta.shape
    width = wide // 8
    return pl.pallas_call(
        scale_kernel,
        out_shape=[jax.ShapeDtypeStruct((2, rows, width), jnp.bfloat16)] * 4,
        in_specs=[pl.BlockSpec(memory_space=pltpu.VMEM)] * 2,
        out_specs=[pl.BlockSpec(memory_space=pltpu.HBM)] * 4,
        scratch_shapes=[pltpu.VMEM((8, rows, width), jnp.bfloat16), pltpu.SemaphoreType.DMA((8,))],
        compiler_params=pltpu.CompilerParams(vmem_limit_bytes=SCOPED),
        cost_estimate=FREE,
        name="scaled_delta",
    )(exps, delta)


def refresh_kernel(other_hi, same, other, base, out, held, sem):
    x, z_lo, y, z_hi, core = position()
    owner = lax.rem(z_hi + other_hi, 2) * 8 + y * 2 + core
    copy = pltpu.make_async_copy(base.at[pl.ds(owner * 8, 8)], held, sem)
    copy.start()
    copy.wait()
    for t in range(8):
        j = lax.rem(x - t // 2 + 4, 4)
        delta = jnp.where(z_lo == t % 2, same[j].astype(jnp.float32), other[j].astype(jnp.float32))
        out[t] = (held[t].astype(jnp.float32) + delta).astype(jnp.bfloat16)


def refresh(same, other, base, other_hi, name):
    shape = (8, *base.shape[1:])
    vmem = pl.BlockSpec(memory_space=pltpu.VMEM)
    out = pl.pallas_call(
        functools.partial(refresh_kernel, other_hi),
        out_shape=jax.ShapeDtypeStruct(shape, jnp.bfloat16),
        in_specs=[vmem, vmem, pl.BlockSpec(memory_space=pltpu.HBM)],
        out_specs=vmem,
        scratch_shapes=[pltpu.VMEM(shape, jnp.bfloat16), pltpu.SemaphoreType.DMA],
        compiler_params=pltpu.CompilerParams(vmem_limit_bytes=SCOPED),
        cost_estimate=FREE,
        name=name,
    )(same, other, base)
    return out.reshape(8 * shape[1], shape[2])


def gate(*values):
    return lax.optimization_barrier(values)


STEPS = (0, -1, 1, 2)
TILE = 256
HBM = pl.BlockSpec(memory_space=pltpu.HBM)
VMEM = pl.BlockSpec(memory_space=pltpu.VMEM)


def silu(hidden):
    return hidden / (1.0 + jnp.exp(-hidden))


def start_weights(block, held, pieces, spots, sem):
    _, _, y, z_hi, core = position()
    piece = held.shape[0] // 4
    for which, step, other_core, other_hi in spots:
        y2 = lax.rem(y + step + 4, 4)
        part = lax.rem(y2, 2) * 2 + lax.rem(core + other_core, 2)

        @pl.when(lax.rem(z_hi + other_hi, 2) * 2 + y2 // 2 == block)
        def _(which=which, part=part):
            target = held.at[pl.ds(pl.multiple_of(part * piece, 16), piece)]
            pltpu.make_async_copy(pieces[which], target, sem).start()


def start_tokens(held, pieces, spots, sem):
    z_lo = position()[1]
    half = held.shape[1] // 2
    for which, row, side, first, size in spots:
        column = jnp.where(z_lo == 0, side, 1 - side)
        target = held.at[pl.ds(row, size), pl.ds(pl.multiple_of(column * half, 128), half)]
        pltpu.make_async_copy(pieces[which].at[pl.ds(first, size)], target, sem).start()


def wait_all(held, sem):
    pltpu.make_async_copy(held, held, sem).wait()


def tile_spots(spots, i):
    parts = []
    for which, row, side, first, size in spots:
        low, high = max(row, i * TILE), min(row + size, (i + 1) * TILE)
        if low < high:
            parts.append((which, low, side, first + low - row, high - low))
    return parts


def product_kernel(n_tok, n_wt, token_spots, weight_spots, *refs):
    tokens, weights = refs[:n_tok], refs[n_tok : n_tok + n_wt]
    out, xbuf, wbuf, acc, xsem, wsem, asem = refs[n_tok + n_wt :]
    x = position()[0]
    tiles = acc.shape[0] // TILE

    def start(j):
        start_weights(lax.rem(x + STEPS[j] + 4, 4), wbuf.at[j], weights, weight_spots, wsem.at[j])
        for i in range(tiles):
            start_tokens(xbuf.at[j], tokens, tile_spots(token_spots[j], i), xsem.at[j, i])

    start(0)
    for j in range(3):
        wait_all(wbuf.at[j], wsem.at[j])
        if j < 2:
            start(j + 1)

        @pl.loop(0, tiles)
        def _(i, j=j):
            here = pl.ds(pl.multiple_of(i * TILE, TILE), TILE)
            wait_all(xbuf.at[j, here], xsem.at[j, i])
            part = jnp.dot(xbuf[j, here], wbuf[j], preferred_element_type=jnp.float32)
            if j == 0:
                acc[here] = part
            else:
                acc[here] += part
            if j == 2:
                pltpu.make_async_copy(acc.at[here], out.at[here], asem).start()

    pltpu.make_async_copy(acc, out, asem).wait()


def product(tokens, token_spots, weights, weight_spots, rows, depth):
    width = weights[0].shape[-1]
    operands = [*tokens, *weights]
    return pl.pallas_call(
        functools.partial(product_kernel, len(tokens), len(weights), token_spots, weight_spots),
        out_shape=jax.ShapeDtypeStruct((rows, width), jnp.float32),
        in_specs=[HBM] * len(operands),
        out_specs=HBM,
        scratch_shapes=[
            pltpu.VMEM((3, rows, depth), jnp.bfloat16),
            pltpu.VMEM((3, depth, width), jnp.bfloat16),
            pltpu.VMEM((rows, width), jnp.float32),
            pltpu.SemaphoreType.DMA((3, rows // TILE)),
            pltpu.SemaphoreType.DMA((3,)),
            pltpu.SemaphoreType.DMA,
        ],
        compiler_params=pltpu.CompilerParams(vmem_limit_bytes=SCOPED),
        cost_estimate=FREE,
        name="product_most",
    )(*operands)


def finish_kernel(n_tok, n_wt, token_spots, weight_spots, *refs):
    tokens, weights = refs[:n_tok], refs[n_tok : n_tok + n_wt]
    inv, before, out, xbuf, wbuf, acc, result, xsem, wsem, asem, osem = refs[n_tok + n_wt :]
    x = position()[0]
    start_weights(lax.rem(x + 2, 4), wbuf, weights, weight_spots, wsem)
    tiles = acc.shape[0] // TILE
    loads = []
    for i in range(tiles):
        spots = tile_spots(token_spots, i)
        start_tokens(xbuf, tokens, spots, xsem.at[i])
        here = pl.ds(i * TILE, TILE)
        loads.append(pltpu.make_async_copy(before.at[here], acc.at[here], asem.at[i]))
        loads[i].start()
    wait_all(wbuf, wsem)
    stores = []
    for i in range(tiles):
        here = pl.ds(i * TILE, TILE)
        wait_all(xbuf.at[here], xsem.at[i])
        loads[i].wait()
        part = jnp.dot(xbuf[here], wbuf[...], preferred_element_type=jnp.float32)
        result[here] = silu((acc[here] + part) * inv[here]).astype(out.dtype)
        stores.append(pltpu.make_async_copy(result.at[here], out.at[here], osem.at[i]))
        stores[i].start()
    for store in stores:
        store.wait()


def finish(tokens, token_spots, weights, weight_spots, inv, before, depth):
    rows, width = before.shape
    return pl.pallas_call(
        functools.partial(finish_kernel, len(tokens), len(weights), token_spots, weight_spots),
        out_shape=jax.ShapeDtypeStruct((rows, width), jnp.bfloat16),
        in_specs=[HBM] * (len(tokens) + len(weights)) + [VMEM, HBM],
        out_specs=HBM,
        scratch_shapes=[
            pltpu.VMEM((rows, depth), jnp.bfloat16),
            pltpu.VMEM((depth, width), jnp.bfloat16),
            pltpu.VMEM((rows, width), jnp.float32),
            pltpu.VMEM((rows, width), jnp.bfloat16),
            pltpu.SemaphoreType.DMA((rows // TILE,)),
            pltpu.SemaphoreType.DMA,
            pltpu.SemaphoreType.DMA((rows // TILE,)),
            pltpu.SemaphoreType.DMA((rows // TILE,)),
        ],
        compiler_params=pltpu.CompilerParams(vmem_limit_bytes=SCOPED),
        cost_estimate=FREE,
        name="product_rest",
    )(*tokens, *weights, inv, before)


def packed(square, columns):
    lead = lax.reduce_precision(square, 8, 7)
    fill = jnp.zeros((2 * columns - square.shape[0],), jnp.float32)
    flat = jnp.concatenate([lead, fill, square - lead, fill]).reshape(4, columns)
    return jnp.concatenate([flat, jnp.zeros((12, columns), jnp.float32)], axis=0).astype(jnp.bfloat16)


def local(tokens, gain, rollout_weight, delta_values, scale_exponents):
    count, features = tokens.shape
    total = features * 8
    block, width = rollout_weight.shape[0] // 16, rollout_weight.shape[1]
    base = rollout_weight.reshape(128, block // 8, width)
    n_a, n_b, n_c = count // 4, 7 * count // 16, 5 * count // 16
    at_b, at_c, extra = n_a, n_a + n_b, 16
    depth = 2 * features

    parts = scaled_delta(scale_exponents, delta_values)
    got = [parts[0]] + [shift(parts[j], x=j) for j in (1, 2, 3)]
    values = tokens.astype(jnp.float32)
    scaled = (values * gain[None, :]).astype(jnp.bfloat16)
    square = jnp.sum(values * values, axis=1)
    mine_a = jnp.concatenate([scaled[:n_a], packed(square, features)], axis=0)
    mine_b, mine_c = scaled[at_b:at_c], scaled[at_c:]
    mine_a, *_ = gate(mine_a, *parts)
    theirs_a = shift(mine_a, z_lo=1)

    got[1], got[2], got[3], mine_c = gate(got[1], got[2], got[3], mine_c)
    same = jnp.stack([g[0] for g in got])
    other = jnp.stack([g[1] for g in got])
    near, across = shift(other, z_lo=1), shift(other, z_lo=1, z_hi=1)
    left_c, right_c = shift(mine_c, x=1), shift(mine_c, x=-1)

    pair_a = jnp.concatenate([mine_a, theirs_a], axis=0)
    near, across, left_c, right_c, same_z, pair_a = gate(near, across, left_c, right_c, same, pair_a)
    left_a, right_a = shift(pair_a, x=1), shift(pair_a, x=-1)
    far = shift(same_z, z_hi=1)
    own = refresh(same, near, base, 0, "refresh_own")
    own_l, own_r = shift(own, y=1), shift(own, y=-1)
    mine_bz, far = gate(mine_b, far)
    theirs_b = shift(mine_bz, z_lo=1)
    other_hi = refresh(far, across, base, 1, "refresh_far")

    left_a, right_a, right_c = gate(left_a, right_a, right_c)
    opposite_a, opposite_c = shift(left_a, x=1), shift(right_c, x=-1)
    other_hi, left_a, right_a, own_l, own_r = gate(other_hi, left_a, right_a, own_l, own_r)
    far_l, far_r = shift(other_hi, y=1), shift(other_hi, y=-1)
    pair_b = jnp.concatenate([mine_b, theirs_b], axis=0)
    pair_b, opposite_a, opposite_c = gate(pair_b, opposite_a, opposite_c)
    left_b, right_b = shift(pair_b, x=1), shift(pair_b, x=-1)
    three_c, theirs_b = gate(jnp.concatenate([mine_c, left_c, right_c], axis=0), theirs_b)
    theirs_c = shift(three_c, z_lo=1)
    tail = sum(
        v[at : at + 4].astype(jnp.float32)
        for v in (pair_a, left_a, right_a, opposite_a)
        for at in (n_a, 2 * n_a + extra)
    ).reshape(2, 2 * features)
    inv = lax.rsqrt((tail[0] + tail[1])[:count] / total + 1e-06)[:, None]
    own_lf, far_l, far_r, inv = gate(own_l, far_l, far_r, inv)
    own_o, far_o = shift(own_lf, y=1), shift(far_r, y=-1)
    rings = [own, own_l, own_r, other_hi, far_l, far_r]
    swaps = [shift(v, core=1) for v in rings]

    left_b, right_b, theirs_c, own_o, far_o = gate(left_b, right_b, theirs_c, own_o, far_o)
    cut = (2 * n_b - n_c) // 32 * 16
    up = shift(jnp.concatenate([theirs_c[n_c : 2 * n_c], left_b[:cut]], axis=0), x=1)
    down = shift(right_b[cut:], x=-1)

    tokens_all = [pair_a, left_a, right_a, pair_b, left_b, right_b, mine_c, left_c, right_c, theirs_c]
    token_spots = []
    for j in range(3):
        spots = [(j, 0, side, side * (n_a + extra), n_a) for side in (0, 1)]
        spots += [(3 + j, at_b, side, side * n_b, n_b) for side in (0, 1)]
        token_spots.append(spots + [(6 + j, at_c, 0, 0, n_c), (9, at_c, 1, j * n_c, n_c)])
    weights = [*rings, *swaps, own_o, far_o, shift(own_o, core=1), shift(far_o, core=1)]
    weight_spots = [(6 * c + 3 * hi + k, STEPS[k], c, hi) for c in (0, 1) for hi in (0, 1) for k in range(3)]
    weight_spots += [(12 + 2 * c + hi, 2, c, hi) for c in (0, 1) for hi in (0, 1)]
    partial = product(tokens_all, token_spots, weights, weight_spots, count, depth)

    spots = [(0, 0, side, side * (n_a + extra), n_a) for side in (0, 1)]
    spots += [(1, at_c, 0, 0, n_c), (2, at_c, 1, 0, n_c)]
    spots += [(2, at_b, 0, n_c, cut), (3, at_b + cut, 0, 0, n_b - cut), (3, at_b, 1, n_b - cut, n_b)]
    return finish([opposite_a, opposite_c, up, down], spots, weights, weight_spots, inv, partial, depth)


def solution(mesh):
    in_specs = (
        P("fsdp", "tp"),
        P("tp"),
        P(None, "tp"),
        P(("fsdp", "tp"), None),
        P(("fsdp", "tp"), None),
    )
    out_specs = P("fsdp", "tp")
    return jax.shard_map(local, mesh=mesh, in_specs=in_specs, out_specs=out_specs, check_vma=False)
```

```python
import functools

import jax
import jax.numpy as jnp
from jax import lax
from jax.experimental import pallas as pl
from jax.experimental.pallas import tpu as pltpu
from jax.sharding import PartitionSpec as P


SCOPED = 60 * 2**20
FREE = pl.CostEstimate(flops=0, bytes_accessed=0, transcendentals=0)


def links(x=0, z_lo=0, z_hi=0, y=0, core=0):
    pairs = []
    for f in range(16):
        for t in range(8):
            f2 = (((f // 8) + z_hi) % 2) * 8 + (((f // 2) % 4 + y) % 4) * 2 + (f + core) % 2
            t2 = ((t // 2 + x) % 4) * 2 + (t + z_lo) % 2
            pairs.append((f * 8 + t, f2 * 8 + t2))
    return pairs


def shift(value, **step):
    return lax.ppermute(value, ("fsdp", "tp"), links(**step))


def position():
    f, t = lax.axis_index("fsdp"), lax.axis_index("tp")
    return t // 2, t % 2, (f // 2) % 4, f // 8, f % 2


def power_two(exps):
    total = jnp.zeros(exps.shape, jnp.float32)
    for level in range(-8, -4):
        total = total + jnp.where(exps == level, jnp.float32(2.0**level), jnp.float32(0.0))
    return total


def scale_kernel(exps, delta, *refs):
    outs, held, sems = refs[:4], refs[4], refs[5]
    scale = power_two(exps[...])
    x, z_lo, _, _, _ = position()
    width = held.shape[2]
    for g in range(exps.shape[1]):
        piece = delta[:, g * 128 : (g + 1) * 128].astype(jnp.float32) * scale[:, g : g + 1]
        owner, at = divmod(g * 128, width)
        held[owner, :, at : at + 128] = piece.astype(jnp.bfloat16)
    copies = []
    for j in range(4):
        for half in (0, 1):
            owner = lax.rem(x + j, 4) * 2 + (z_lo if half == 0 else 1 - z_lo)
            copies.append(pltpu.make_async_copy(held.at[owner], outs[j].at[half], sems.at[2 * j + half]))
            copies[-1].start()
    for copy in copies:
        copy.wait()


def scaled_delta(exps, delta):
    rows, wide = delta.shape
    width = wide // 8
    return pl.pallas_call(
        scale_kernel,
        out_shape=[jax.ShapeDtypeStruct((2, rows, width), jnp.bfloat16)] * 4,
        in_specs=[pl.BlockSpec(memory_space=pltpu.VMEM)] * 2,
        out_specs=[pl.BlockSpec(memory_space=pltpu.HBM)] * 4,
        scratch_shapes=[pltpu.VMEM((8, rows, width), jnp.bfloat16), pltpu.SemaphoreType.DMA((8,))],
        compiler_params=pltpu.CompilerParams(vmem_limit_bytes=SCOPED),
        cost_estimate=FREE,
        name="scaled_delta",
    )(exps, delta)


def refresh_kernel(other_hi, same, other, base, out, held, sem):
    x, z_lo, y, z_hi, core = position()
    owner = lax.rem(z_hi + other_hi, 2) * 8 + y * 2 + core
    copy = pltpu.make_async_copy(base.at[pl.ds(owner * 8, 8)], held, sem)
    copy.start()
    copy.wait()
    for t in range(8):
        j = lax.rem(x - t // 2 + 4, 4)
        delta = jnp.where(z_lo == t % 2, same[j].astype(jnp.float32), other[j].astype(jnp.float32))
        out[t] = (held[t].astype(jnp.float32) + delta).astype(jnp.bfloat16)


def refresh(same, other, base, other_hi, name):
    shape = (8, *base.shape[1:])
    vmem = pl.BlockSpec(memory_space=pltpu.VMEM)
    out = pl.pallas_call(
        functools.partial(refresh_kernel, other_hi),
        out_shape=jax.ShapeDtypeStruct(shape, jnp.bfloat16),
        in_specs=[vmem, vmem, pl.BlockSpec(memory_space=pltpu.HBM)],
        out_specs=vmem,
        scratch_shapes=[pltpu.VMEM(shape, jnp.bfloat16), pltpu.SemaphoreType.DMA],
        compiler_params=pltpu.CompilerParams(vmem_limit_bytes=SCOPED),
        cost_estimate=FREE,
        name=name,
    )(same, other, base)
    return out.reshape(8 * shape[1], shape[2])


def gate(*values):
    return lax.optimization_barrier(values)


STEPS = (0, -1, 1, 2)
TILE = 256
HBM = pl.BlockSpec(memory_space=pltpu.HBM)
VMEM = pl.BlockSpec(memory_space=pltpu.VMEM)


def silu(hidden):
    half = 0.5 * hidden
    return half + half * jnp.tanh(half)


def start_weights(block, held, pieces, spots, sem):
    _, _, y, z_hi, core = position()
    piece = held.shape[0] // 4
    for which, step, other_core, other_hi in spots:
        y2 = lax.rem(y + step + 4, 4)
        part = lax.rem(y2, 2) * 2 + lax.rem(core + other_core, 2)

        @pl.when(lax.rem(z_hi + other_hi, 2) * 2 + y2 // 2 == block)
        def _(which=which, part=part):
            target = held.at[pl.ds(pl.multiple_of(part * piece, 16), piece)]
            pltpu.make_async_copy(pieces[which], target, sem).start()


def start_tokens(held, pieces, spots, sem):
    z_lo = position()[1]
    half = held.shape[1] // 2
    for which, row, side, first, size in spots:
        column = jnp.where(z_lo == 0, side, 1 - side)
        target = held.at[pl.ds(row, size), pl.ds(pl.multiple_of(column * half, 128), half)]
        pltpu.make_async_copy(pieces[which].at[pl.ds(first, size)], target, sem).start()


def wait_all(held, sem):
    pltpu.make_async_copy(held, held, sem).wait()


def tile_spots(spots, i):
    parts = []
    for which, row, side, first, size in spots:
        low, high = max(row, i * TILE), min(row + size, (i + 1) * TILE)
        if low < high:
            parts.append((which, low, side, first + low - row, high - low))
    return parts


def product_kernel(n_tok, n_wt, token_spots, weight_spots, *refs):
    tokens, weights = refs[:n_tok], refs[n_tok : n_tok + n_wt]
    out, xbuf, wbuf, acc, xsem, wsem, asem = refs[n_tok + n_wt :]
    x = position()[0]
    tiles = acc.shape[0] // TILE

    def start(j):
        start_weights(lax.rem(x + STEPS[j] + 4, 4), wbuf.at[j], weights, weight_spots, wsem.at[j])
        for i in range(tiles):
            start_tokens(xbuf.at[j], tokens, tile_spots(token_spots[j], i), xsem.at[j, i])

    start(0)
    for j in range(3):
        wait_all(wbuf.at[j], wsem.at[j])
        if j < 2:
            start(j + 1)

        @pl.loop(0, tiles)
        def _(i, j=j):
            here = pl.ds(pl.multiple_of(i * TILE, TILE), TILE)
            wait_all(xbuf.at[j, here], xsem.at[j, i])
            part = jnp.dot(xbuf[j, here], wbuf[j], preferred_element_type=jnp.float32)
            if j == 0:
                acc[here] = part
            else:
                acc[here] += part
            if j == 2:
                pltpu.make_async_copy(acc.at[here], out.at[here], asem).start()

    pltpu.make_async_copy(acc, out, asem).wait()


def product(tokens, token_spots, weights, weight_spots, rows, depth):
    width = weights[0].shape[-1]
    operands = [*tokens, *weights]
    return pl.pallas_call(
        functools.partial(product_kernel, len(tokens), len(weights), token_spots, weight_spots),
        out_shape=jax.ShapeDtypeStruct((rows, width), jnp.float32),
        in_specs=[HBM] * len(operands),
        out_specs=HBM,
        scratch_shapes=[
            pltpu.VMEM((3, rows, depth), jnp.bfloat16),
            pltpu.VMEM((3, depth, width), jnp.bfloat16),
            pltpu.VMEM((rows, width), jnp.float32),
            pltpu.SemaphoreType.DMA((3, rows // TILE)),
            pltpu.SemaphoreType.DMA((3,)),
            pltpu.SemaphoreType.DMA,
        ],
        compiler_params=pltpu.CompilerParams(vmem_limit_bytes=SCOPED),
        cost_estimate=FREE,
        name="product_most",
    )(*operands)


def finish_kernel(n_tok, n_wt, token_spots, weight_spots, *refs):
    tokens, weights = refs[:n_tok], refs[n_tok : n_tok + n_wt]
    inv, before, out, xbuf, wbuf, acc, result, xsem, wsem, asem, osem = refs[n_tok + n_wt :]
    x = position()[0]
    start_weights(lax.rem(x + 2, 4), wbuf, weights, weight_spots, wsem)
    tiles = acc.shape[0] // TILE
    loads = []
    for i in range(tiles):
        spots = tile_spots(token_spots, i)
        start_tokens(xbuf, tokens, spots, xsem.at[i])
        here = pl.ds(i * TILE, TILE)
        loads.append(pltpu.make_async_copy(before.at[here], acc.at[here], asem.at[i]))
        loads[i].start()
    wait_all(wbuf, wsem)
    stores = []
    for i in range(tiles):
        here = pl.ds(i * TILE, TILE)
        wait_all(xbuf.at[here], xsem.at[i])
        loads[i].wait()
        part = jnp.dot(xbuf[here], wbuf[...], preferred_element_type=jnp.float32)
        result[here] = silu((acc[here] + part) * inv[here, 0:1]).astype(out.dtype)
        stores.append(pltpu.make_async_copy(result.at[here], out.at[here], osem.at[i]))
        stores[i].start()
    for store in stores:
        store.wait()


def finish(tokens, token_spots, weights, weight_spots, inv, before, depth):
    rows, width = before.shape
    return pl.pallas_call(
        functools.partial(finish_kernel, len(tokens), len(weights), token_spots, weight_spots),
        out_shape=jax.ShapeDtypeStruct((rows, width), jnp.bfloat16),
        in_specs=[HBM] * (len(tokens) + len(weights)) + [VMEM, HBM],
        out_specs=HBM,
        scratch_shapes=[
            pltpu.VMEM((rows, depth), jnp.bfloat16),
            pltpu.VMEM((depth, width), jnp.bfloat16),
            pltpu.VMEM((rows, width), jnp.float32),
            pltpu.VMEM((rows, width), jnp.bfloat16),
            pltpu.SemaphoreType.DMA((rows // TILE,)),
            pltpu.SemaphoreType.DMA,
            pltpu.SemaphoreType.DMA((rows // TILE,)),
            pltpu.SemaphoreType.DMA((rows // TILE,)),
        ],
        compiler_params=pltpu.CompilerParams(vmem_limit_bytes=SCOPED),
        cost_estimate=FREE,
        name="product_rest",
    )(*tokens, *weights, inv, before)


def packed(square, columns):
    lead = lax.reduce_precision(square, 8, 7)
    fill = jnp.zeros((2 * columns - square.shape[0],), jnp.float32)
    flat = jnp.concatenate([lead, fill, square - lead, fill]).reshape(4, columns)
    return jnp.concatenate([flat, jnp.zeros((12, columns), jnp.float32)], axis=0).astype(jnp.bfloat16)


def local(tokens, gain, rollout_weight, delta_values, scale_exponents):
    count, features = tokens.shape
    total = features * 8
    block, width = rollout_weight.shape[0] // 16, rollout_weight.shape[1]
    base = rollout_weight.reshape(128, block // 8, width)
    n_a, n_b, n_c = count // 4, 7 * count // 16, 5 * count // 16
    at_b, at_c, extra = n_a, n_a + n_b, 16
    depth = 2 * features

    parts = scaled_delta(scale_exponents, delta_values)
    got = [parts[0]] + [shift(parts[j], x=j) for j in (1, 2, 3)]
    values = tokens.astype(jnp.float32)
    scaled = (values * gain[None, :]).astype(jnp.bfloat16)
    square = jnp.sum(values * values, axis=1)
    mine_a = jnp.concatenate([scaled[:n_a], packed(square, features)], axis=0)
    mine_b, mine_c = scaled[at_b:at_c], scaled[at_c:]
    mine_a, *_ = gate(mine_a, *parts)
    theirs_a = shift(mine_a, z_lo=1)

    got[1], got[2], got[3], mine_c = gate(got[1], got[2], got[3], mine_c)
    same = jnp.stack([g[0] for g in got])
    other = jnp.stack([g[1] for g in got])
    near, across = shift(other, z_lo=1), shift(other, z_lo=1, z_hi=1)
    left_c, right_c = shift(mine_c, x=1), shift(mine_c, x=-1)

    pair_a = jnp.concatenate([mine_a, theirs_a], axis=0)
    near, across, left_c, right_c, same_z, pair_a = gate(near, across, left_c, right_c, same, pair_a)
    left_a, right_a = shift(pair_a, x=1), shift(pair_a, x=-1)
    far = shift(same_z, z_hi=1)
    own = refresh(same, near, base, 0, "refresh_own")
    own_l, own_r = shift(own, y=1), shift(own, y=-1)
    mine_bz, far = gate(mine_b, far)
    theirs_b = shift(mine_bz, z_lo=1)
    other_hi = refresh(far, across, base, 1, "refresh_far")

    left_a, right_a, right_c = gate(left_a, right_a, right_c)
    opposite_a, opposite_c = shift(left_a, x=1), shift(right_c, x=-1)
    other_hi, left_a, right_a, own_l, own_r = gate(other_hi, left_a, right_a, own_l, own_r)
    far_l, far_r = shift(other_hi, y=1), shift(other_hi, y=-1)
    pair_b = jnp.concatenate([mine_b, theirs_b], axis=0)
    pair_b, opposite_a, opposite_c = gate(pair_b, opposite_a, opposite_c)
    left_b, right_b = shift(pair_b, x=1), shift(pair_b, x=-1)
    three_c, theirs_b = gate(jnp.concatenate([mine_c, left_c, right_c], axis=0), theirs_b)
    theirs_c = shift(three_c, z_lo=1)
    tail = sum(
        v[at : at + 4].astype(jnp.float32)
        for v in (pair_a, left_a, right_a, opposite_a)
        for at in (n_a, 2 * n_a + extra)
    ).reshape(2, 2 * features)
    inv = jnp.broadcast_to(lax.rsqrt((tail[0] + tail[1])[:count] / total + 1e-06)[:, None], (count, 128))
    own_lf, far_l, far_r, inv = gate(own_l, far_l, far_r, inv)
    own_o, far_o = shift(own_lf, y=1), shift(far_r, y=-1)
    rings = [own, own_l, own_r, other_hi, far_l, far_r]
    swaps = [shift(v, core=1) for v in rings]

    left_b, right_b, theirs_c, own_o, far_o = gate(left_b, right_b, theirs_c, own_o, far_o)
    cut = (2 * n_b - n_c) // 32 * 16
    up = shift(jnp.concatenate([theirs_c[n_c : 2 * n_c], left_b[:cut]], axis=0), x=1)
    down = shift(right_b[cut:], x=-1)

    tokens_all = [pair_a, left_a, right_a, pair_b, left_b, right_b, mine_c, left_c, right_c, theirs_c]
    token_spots = []
    for j in range(3):
        spots = [(j, 0, side, side * (n_a + extra), n_a) for side in (0, 1)]
        spots += [(3 + j, at_b, side, side * n_b, n_b) for side in (0, 1)]
        token_spots.append(spots + [(6 + j, at_c, 0, 0, n_c), (9, at_c, 1, j * n_c, n_c)])
    weights = [*rings, *swaps, own_o, far_o, shift(own_o, core=1), shift(far_o, core=1)]
    weight_spots = [(6 * c + 3 * hi + k, STEPS[k], c, hi) for c in (0, 1) for hi in (0, 1) for k in range(3)]
    weight_spots += [(12 + 2 * c + hi, 2, c, hi) for c in (0, 1) for hi in (0, 1)]
    partial = product(tokens_all, token_spots, weights, weight_spots, count, depth)

    spots = [(0, 0, side, side * (n_a + extra), n_a) for side in (0, 1)]
    spots += [(1, at_c, 0, 0, n_c), (2, at_c, 1, 0, n_c)]
    spots += [(2, at_b, 0, n_c, cut), (3, at_b + cut, 0, 0, n_b - cut), (3, at_b, 1, n_b - cut, n_b)]
    return finish([opposite_a, opposite_c, up, down], spots, weights, weight_spots, inv, partial, depth)


def solution(mesh):
    in_specs = (
        P("fsdp", "tp"),
        P("tp"),
        P(None, "tp"),
        P(("fsdp", "tp"), None),
        P(("fsdp", "tp"), None),
    )
    out_specs = P("fsdp", "tp")
    return jax.shard_map(local, mesh=mesh, in_specs=in_specs, out_specs=out_specs, check_vma=False)
```
